128 devices in a mesh: ctx: 64 (over x_hi, z, y, core), head: 2 (over x_lo).
Axes of the slice: x: 4 (x_hi: 2, x_lo: 2; x = x_hi * 2 + x_lo), y: 4, z: 4, core: 2. Of those that a mesh axis runs over, the one named last changes fastest.
Arguments:
- hidden_states: bfloat16 [32768, 5376], P('ctx', 'head'), may hold values from -6 to 6
- query_base: bfloat16 [32768, 4096], P('ctx', 'head'), may hold values from -8 to 8
- key_base: bfloat16 [32768, 2048], P('ctx', 'head'), may hold values from -8 to 8
- frozen_value_rows: bfloat16 [32768, 2048], P('ctx', 'head'), may hold values from -6 to 6
- query_down: bfloat16 [5376, 16], P('head'), may hold values from -0.078125 to 0.078125
- query_up: bfloat16 [16, 4096], P(None, 'head'), may hold values from -0.75 to 0.75
- value_down: bfloat16 [5376, 16], P('head'), may hold values from -0.078125 to 0.078125
- value_up_weight: bfloat16 [16, 2048], P(None, 'head'), may hold values from -0.75 to 0.75
- positions: int32 [32768], P('ctx'), may hold values from 0 to 65534, as said below
- block_mask: int32 [256, 9], replicated, may hold values from 0 to 1, as said below
- output_gradient: bfloat16 [32768, 4096], P('ctx', 'head'), may hold values from -96 to 96
Outputs:
- attention_out: bfloat16 [32768, 4096], P('ctx', 'head')
- grad_query_down: float32 [5376, 16], P('head')
- grad_query_up: float32 [16, 4096], P(None, 'head')
- grad_value_down: float32 [5376, 16], P('head')
- grad_value_up: float32 [16, 2048], P(None, 'head')
The draws below stay inside these ranges and needn't reach their ends.
Inputs may be any that keep to these rules, and one draw needn't show every extreme that they name: positions rise strictly along the tokens. `block_mask`: entry (b, o) is 1 where the query block b may attend the key block b - o; column 0 is 1 in every row.
All inputs are finite; a program needn't handle non-finite values.
Results may differ from the reference program's by a relative error of at most 0.04.
Values may be sent and summed in bfloat16 or wider, within the bound.
A program may use at most 192 MiB of HBM per device.

```python
import jax
import jax.numpy as jnp
from jax import lax

D = 5376
QUERY_HEADS = 32
KEY_VALUE_HEADS = 16
HEAD_SIZE = 128
WINDOW = 1024
ADAPTER_RANK = 16
BLOCK = 128
TOK_DEV = 512
DOCUMENT_TOKENS = 32768
NBLK = 256
BAND = 9


def position_table(key):
    skips = jax.random.randint(jax.random.fold_in(key, 7), (DOCUMENT_TOKENS,), 0, 2).astype(jnp.int32)
    token_ids = jnp.arange(DOCUMENT_TOKENS, dtype=jnp.int32)
    rising = (token_ids + jnp.cumsum(skips).astype(jnp.int32) - skips[0]).astype(jnp.int32)
    return jnp.where(token_ids == DOCUMENT_TOKENS - 1, 2 * DOCUMENT_TOKENS - 2, rising).astype(jnp.int32)


def draw_positions(key, part):
    return position_table(key)


def draw_block_mask(key, part):
    coins = jax.random.randint(jax.random.fold_in(key, 53), (NBLK, BAND), 0, 4)
    column = jnp.arange(BAND, dtype=jnp.int32)[None, :]
    return jnp.where(column == 0, 1, (coins > 0).astype(jnp.int32)).astype(jnp.int32)


def draw_key_base(key, part):
    unadapted_result = jnp.clip(jax.random.normal(jax.random.fold_in(key, 41), (DOCUMENT_TOKENS, KEY_VALUE_HEADS * HEAD_SIZE), jnp.float32), -6.0, 6.0)
    return unadapted_result.astype(jnp.bfloat16)


def draw_query_base(key, part):
    unadapted_result = jnp.clip(jax.random.normal(jax.random.fold_in(key, 45), (DOCUMENT_TOKENS, QUERY_HEADS * HEAD_SIZE), jnp.float32), -6.0, 6.0)
    return unadapted_result.astype(jnp.bfloat16)


def block_scale(stream_key, dims, pieces, smallest, top_value):
    gain, own = 1.0, jax.random.fold_in(stream_key, 6)
    for dim, shards_of in pieces:
        draws = jnp.exp(jax.random.uniform(jax.random.fold_in(own, dim), (shards_of,), jnp.float32, smallest / len(pieces), top_value / len(pieces)))
        gain = gain * jnp.repeat(draws, dims[dim] // shards_of).reshape([-1 if axis == dim else 1 for axis in range(len(dims))])
    return gain


def bell_draw(own_key, dims, width, limit, split=(), kind=jnp.bfloat16):
    drawn = jax.random.normal(own_key, dims, jnp.float32) * width
    if len(split) > 0:
        drawn = block_scale(own_key, dims, split, -0.22, 0.18) * drawn
    return jnp.clip(drawn, min=-limit, max=limit).astype(kind)


def setup_inputs(seed: int = 0) -> dict:
    key_list = jax.random.split(jax.random.key(seed), 12)
    return {
        "hidden_states": bell_draw(key_list[0], (DOCUMENT_TOKENS, D), 1.0, 6.0, ((0, 64), (1, 2))),
        "query_base": draw_query_base(jax.random.fold_in(key_list[11], 71), 0),
        "key_base": draw_key_base(jax.random.fold_in(key_list[11], 71), 0),
        "frozen_value_rows": bell_draw(key_list[3], (DOCUMENT_TOKENS, KEY_VALUE_HEADS * HEAD_SIZE), 1.0, 6.0, ((0, 64), (1, 2))),
        "query_down": bell_draw(key_list[4], (D, ADAPTER_RANK), D ** -0.5, 0.078125, ((0, 2),)),
        "query_up": bell_draw(key_list[5], (ADAPTER_RANK, QUERY_HEADS * HEAD_SIZE), (4 * ADAPTER_RANK) ** -0.5, 0.75, ((1, 2),)),
        "value_down": bell_draw(key_list[6], (D, ADAPTER_RANK), D ** -0.5, 0.078125, ((0, 2),)),
        "value_up_weight": bell_draw(key_list[7], (ADAPTER_RANK, KEY_VALUE_HEADS * HEAD_SIZE), (4 * ADAPTER_RANK) ** -0.5, 0.75, ((1, 2),)),
        "positions": draw_positions(jax.random.fold_in(key_list[11], 71), 0),
        "block_mask": draw_block_mask(jax.random.fold_in(key_list[11], 71), 0),
        "output_gradient": bell_draw(key_list[10], (DOCUMENT_TOKENS, QUERY_HEADS * HEAD_SIZE), 16.0, 96.0, ((0, 64), (1, 2))),
    }


rope_base = 10000.0


def rotate(row_block, position_ids, turn_sign):
    count = row_block.shape[0]
    col_count = row_block.shape[1]
    half_width = HEAD_SIZE // 2
    frequency = rope_base ** (-(2.0 * jnp.arange(half_width, dtype=jnp.float32)) / HEAD_SIZE)
    angles = position_ids.astype(jnp.float32)[:, None] * frequency[None, :]
    cosines = jnp.concatenate([jnp.cos(angles), jnp.cos(angles)], axis=-1)
    sines = jnp.concatenate([jnp.sin(angles), jnp.sin(angles)], axis=-1)
    shaped = row_block.reshape(count, col_count // HEAD_SIZE, HEAD_SIZE)
    turned = jnp.concatenate([-shaped[..., half_width:], shaped[..., :half_width]], axis=-1)
    return (shaped * cosines[:, None, :] + turn_sign * turned * sines[:, None, :]).reshape(count, col_count)


def allowed_pairs(mask_rows, query_first, key_first, count_of_queries, key_count):
    query_ids = query_first + jnp.arange(count_of_queries, dtype=jnp.int32)
    key_ids = key_first + jnp.arange(key_count, dtype=jnp.int32)
    token_gap = key_ids[None, :] - query_ids[:, None]
    token_ok = (token_gap <= 0) & (token_gap > -WINDOW) & (key_ids >= 0)[None, :]
    query_blocks = query_first // BLOCK + jnp.arange(count_of_queries // BLOCK, dtype=jnp.int32)
    key_blocks = key_first // BLOCK + jnp.arange(key_count // BLOCK, dtype=jnp.int32)
    offset = query_blocks[:, None] - key_blocks[None, :]
    band_size = mask_rows.shape[1]
    band_hit = jnp.any((offset[:, :, None] == jnp.arange(band_size, dtype=jnp.int32)[None, None, :]) & (mask_rows[:, None, :] == 1), axis=-1)
    spread_out = jnp.broadcast_to(band_hit[:, None, :, None], (count_of_queries // BLOCK, BLOCK, key_count // BLOCK, BLOCK)).reshape(count_of_queries, key_count)
    return token_ok & spread_out


def reference(hidden_states, query_base, key_base, frozen_value_rows, query_down, query_up, value_down, value_up_weight, positions, block_mask, output_gradient):
    query_low = jnp.dot(hidden_states, query_down, preferred_element_type=jnp.float32).astype(jnp.bfloat16)
    value_low = jnp.dot(hidden_states, value_down, preferred_element_type=jnp.float32).astype(jnp.bfloat16)
    query_rows = rotate(query_base.astype(jnp.float32) + jnp.dot(query_low, query_up, preferred_element_type=jnp.float32), positions, 1.0).astype(jnp.bfloat16)
    keys = rotate(key_base.astype(jnp.float32), positions, 1.0).astype(jnp.bfloat16)
    values = (frozen_value_rows.astype(jnp.float32) + jnp.dot(value_low, value_up_weight, preferred_element_type=jnp.float32)).astype(jnp.bfloat16)
    count_of_queries = TOK_DEV
    key_extent = WINDOW // TOK_DEV
    key_range_length = (key_extent + 1) * count_of_queries
    query_groups = QUERY_HEADS // KEY_VALUE_HEADS
    score_scale = (D // QUERY_HEADS) ** -0.5
    leading_rows = jnp.zeros((key_extent * count_of_queries, KEY_VALUE_HEADS * HEAD_SIZE), jnp.bfloat16)
    key_rows_padded = jnp.concatenate([leading_rows, keys], axis=0)
    value_rows_padded = jnp.concatenate([leading_rows, values], axis=0)
    block_count = DOCUMENT_TOKENS // count_of_queries

    def block_step(value_sums, block_index):
        leading_token = block_index * count_of_queries
        block_query_rows = lax.dynamic_slice_in_dim(query_rows, leading_token, count_of_queries, 0).reshape(count_of_queries, KEY_VALUE_HEADS, query_groups, HEAD_SIZE).astype(jnp.float32)
        block_gradient_rows = lax.dynamic_slice_in_dim(output_gradient, leading_token, count_of_queries, 0).reshape(count_of_queries, KEY_VALUE_HEADS, query_groups, HEAD_SIZE).astype(jnp.float32)
        block_key_rows = lax.dynamic_slice_in_dim(key_rows_padded, leading_token, key_range_length, 0).reshape(key_range_length, KEY_VALUE_HEADS, HEAD_SIZE).astype(jnp.float32)
        block_value_rows = lax.dynamic_slice_in_dim(value_rows_padded, leading_token, key_range_length, 0).reshape(key_range_length, KEY_VALUE_HEADS, HEAD_SIZE).astype(jnp.float32)
        mask_rows = lax.dynamic_slice_in_dim(block_mask, block_index * (count_of_queries // BLOCK), count_of_queries // BLOCK, 0)
        allowed = allowed_pairs(mask_rows, leading_token, leading_token - key_extent * count_of_queries, count_of_queries, key_range_length)
        scores = jnp.einsum('lhgd,khd->hglk', block_query_rows, block_key_rows) * score_scale
        scores = jnp.where(allowed[None, None], scores, -jnp.inf)
        row_max = jnp.max(scores, axis=-1, keepdims=True)
        log_total = row_max[..., 0] + jnp.log(jnp.sum(jnp.exp(scores - row_max), axis=-1))
        weights = jnp.exp(scores - log_total[..., None])
        rounded_length = weights.astype(jnp.bfloat16)
        block_out = jnp.einsum('hglk,khd->lhgd', rounded_length.astype(jnp.float32), block_value_rows).astype(jnp.bfloat16)
        row_delta = jnp.transpose(jnp.sum(block_gradient_rows * block_out.astype(jnp.float32), axis=-1), (1, 2, 0))
        grad_weights = jnp.einsum('lhgd,khd->hglk', block_gradient_rows, block_value_rows)
        grad_scores = (weights * (grad_weights - row_delta[..., None]) * score_scale).astype(jnp.bfloat16)
        query_part = jnp.einsum('hglk,khd->lhgd', grad_scores.astype(jnp.float32), block_key_rows).reshape(count_of_queries, QUERY_HEADS * HEAD_SIZE)
        value_portion = jnp.einsum('xwzn,zxwy->nxy', rounded_length.astype(jnp.float32), block_gradient_rows).reshape(key_range_length, KEY_VALUE_HEADS * HEAD_SIZE)
        current = lax.dynamic_slice_in_dim(value_sums, leading_token, key_range_length, 0)
        value_sums = lax.dynamic_update_slice_in_dim(value_sums, current + value_portion, leading_token, 0)
        return value_sums, (block_out.reshape(count_of_queries, QUERY_HEADS * HEAD_SIZE), query_part)

    starting_sums = jnp.zeros((DOCUMENT_TOKENS + key_extent * count_of_queries, KEY_VALUE_HEADS * HEAD_SIZE), jnp.float32)
    value_sums, (out_blocks, query_parts) = lax.scan(block_step, starting_sums, jnp.arange(block_count, dtype=jnp.int32))
    attention_out = out_blocks.reshape(DOCUMENT_TOKENS, QUERY_HEADS * HEAD_SIZE)
    query_grad = rotate(query_parts.reshape(DOCUMENT_TOKENS, QUERY_HEADS * HEAD_SIZE), positions, -1.0).astype(jnp.bfloat16)
    value_grad = value_sums[key_extent * count_of_queries:].astype(jnp.bfloat16)
    query_back = jnp.dot(query_grad, query_up.T, preferred_element_type=jnp.float32).astype(jnp.bfloat16)
    value_back = jnp.dot(value_grad, value_up_weight.T, preferred_element_type=jnp.float32).astype(jnp.bfloat16)
    loss_scale = DOCUMENT_TOKENS ** -0.5
    grad_query_down = jnp.dot(hidden_states.T, query_back, preferred_element_type=jnp.float32) * loss_scale
    grad_value_down = jnp.dot(hidden_states.T, value_back, preferred_element_type=jnp.float32) * loss_scale
    grad_query_up = jnp.dot(query_low.T, query_grad, preferred_element_type=jnp.float32) * loss_scale
    grad_value_up = jnp.dot(value_low.T, value_grad, preferred_element_type=jnp.float32) * loss_scale
    return (attention_out, grad_query_down, grad_query_up, grad_value_down, grad_value_up)
```

```python
import functools

import jax
import jax.numpy as jnp
from jax import lax
from jax.experimental import pallas as pl
from jax.experimental.pallas import tpu as pltpu
from jax.sharding import PartitionSpec as P

D = 5376
QUERY_HEADS = 32
KEY_VALUE_HEADS = 16
HEAD_SIZE = 128
WINDOW = 1024
BLOCK = 128


rope_base = 10000.0

RANK = 16
GROUP = 8
CHUNK = 1152
MESH = pl.DeviceIdType.MESH


def pieces_of(widths):
    pieces, start = [], 0
    for which, width in enumerate(widths):
        done = 0
        while done < width:
            chunk, inside = divmod(start + done, CHUNK)
            count = min(width - done, CHUNK - inside)
            pieces.append((which, done, chunk, inside, count))
            done += count
        start += width
    return pieces


def total_kernel(
    widths,
    scale,
    parts,
    o_0,
    o_1,
    o_2,
    o_3,
    near,
    far,
    final,
    near_send,
    near_recv,
    far_send,
    far_recv,
    final_send,
    final_recv,
):
    ctx, head = lax.axis_index("ctx"), lax.axis_index("head")
    member = ctx % GROUP
    group = ctx // GROUP
    near_peers = [group * GROUP + (member + by) % GROUP for by in range(1, GROUP)]
    far_peers = [((group + by) % GROUP) * GROUP + member for by in range(1, GROUP)]

    barrier = pltpu.get_barrier_semaphore()
    for peer in near_peers + far_peers:
        pl.semaphore_signal(barrier, inc=1, device_id=(peer, head), device_id_type=MESH)
    pl.semaphore_wait(barrier, 2 * (GROUP - 1))

    def copy(source, target, send, recv, peer):
        return pltpu.make_async_remote_copy(
            src_ref=source,
            dst_ref=target,
            send_sem=send,
            recv_sem=recv,
            device_id=(peer, head),
            device_id_type=MESH,
        )

    copies = []
    for k, peer in enumerate(near_peers):
        one = copy(
            parts.at[peer % GROUP], near.at[k], near_send.at[k], near_recv.at[k], peer
        )
        one.start()
        copies.append(one)
    total = parts[member].astype(jnp.float32)
    for k, one in enumerate(copies):
        one.wait_recv()
        total += near[k].astype(jnp.float32)
    far[group] = total.astype(jnp.bfloat16)

    far_copies = []
    for k, peer in enumerate(far_peers):
        one = copy(far.at[group], far.at[group], far_send.at[k], far_recv.at[k], peer)
        one.start()
        far_copies.append(one)
    for one in far_copies:
        one.wait_recv()
    total = far[0].astype(jnp.float32)
    for k in range(1, GROUP):
        total += far[k].astype(jnp.float32)
    final[member] = (total * scale).astype(jnp.bfloat16)

    last_copies = []
    for k, peer in enumerate(near_peers):
        one = copy(final.at[member], final.at[member], final_send.at[k], final_recv.at[k], peer)
        one.start()
        last_copies.append(one)
    for one in last_copies:
        one.wait_recv()
    outs = (o_0, o_1, o_2, o_3)
    for which, at, chunk, inside, count in pieces_of(widths):
        outs[which][:, at : at + count] = final[chunk, :, inside : inside + count].astype(
            jnp.float32
        )
    for one in copies + far_copies + last_copies:
        one.wait_send()


def total_over_ctx(parts, widths, scale):
    chunked = (GROUP, RANK, CHUNK)
    return pl.pallas_call(
        functools.partial(total_kernel, widths, scale),
        out_shape=[jax.ShapeDtypeStruct((RANK, width), jnp.float32) for width in widths],
        in_specs=[pl.BlockSpec(memory_space=pltpu.VMEM)],
        out_specs=[pl.BlockSpec(memory_space=pltpu.VMEM)] * len(widths),
        scratch_shapes=[
            pltpu.VMEM((GROUP - 1, RANK, CHUNK), jnp.bfloat16),
            pltpu.VMEM(chunked, jnp.bfloat16),
            pltpu.VMEM(chunked, jnp.bfloat16),
        ]
        + [pltpu.SemaphoreType.DMA((GROUP - 1,))] * 6,
        compiler_params=pltpu.CompilerParams(
            collective_id=0, has_side_effects=True, vmem_limit_bytes=24 * 2**20
        ),
    )(parts)


def shifted(x, axis, by):
    devices = lax.axis_size(axis)
    pairs = [(i, i + by) for i in range(devices) if 0 <= i + by < devices]
    return lax.ppermute(x, axis, pairs)


def rotate(row_block, position_ids, turn_sign):
    count = row_block.shape[0]
    col_count = row_block.shape[1]
    half_width = HEAD_SIZE // 2
    frequency = rope_base ** (-(2.0 * jnp.arange(half_width, dtype=jnp.float32)) / HEAD_SIZE)
    angles = position_ids.astype(jnp.float32)[:, None] * frequency[None, :]
    cosines = jnp.concatenate([jnp.cos(angles), jnp.cos(angles)], axis=-1)
    sines = jnp.concatenate([jnp.sin(angles), jnp.sin(angles)], axis=-1)
    shaped = row_block.reshape(count, col_count // HEAD_SIZE, HEAD_SIZE)
    turned = jnp.concatenate([-shaped[..., half_width:], shaped[..., :half_width]], axis=-1)
    return (shaped * cosines[:, None, :] + turn_sign * turned * sines[:, None, :]).reshape(
        count, col_count
    )


def allowed_pairs(mask_rows, query_first, key_first, count_of_queries, key_count):
    query_ids = query_first + jnp.arange(count_of_queries, dtype=jnp.int32)
    key_ids = key_first + jnp.arange(key_count, dtype=jnp.int32)
    token_gap = key_ids[None, :] - query_ids[:, None]
    token_ok = (token_gap <= 0) & (token_gap > -WINDOW) & (key_ids >= 0)[None, :]
    query_blocks = query_first // BLOCK + jnp.arange(count_of_queries // BLOCK, dtype=jnp.int32)
    key_blocks = key_first // BLOCK + jnp.arange(key_count // BLOCK, dtype=jnp.int32)
    offset = query_blocks[:, None] - key_blocks[None, :]
    band_size = mask_rows.shape[1]
    band_hit = jnp.any(
        (offset[:, :, None] == jnp.arange(band_size, dtype=jnp.int32)[None, None, :])
        & (mask_rows[:, None, :] == 1),
        axis=-1,
    )
    spread_out = jnp.broadcast_to(
        band_hit[:, None, :, None], (count_of_queries // BLOCK, BLOCK, key_count // BLOCK, BLOCK)
    ).reshape(count_of_queries, key_count)
    return token_ok & spread_out


def head_scores(query_rows, key_rows, head_index, score_scale):
    count_of_queries = query_rows.shape[0]
    query_groups = QUERY_HEADS // KEY_VALUE_HEADS
    head_queries = lax.dynamic_slice_in_dim(
        query_rows, head_index * query_groups * HEAD_SIZE, query_groups * HEAD_SIZE, 1
    ).reshape(count_of_queries, query_groups, HEAD_SIZE)
    head_keys = lax.dynamic_slice_in_dim(key_rows, head_index * HEAD_SIZE, HEAD_SIZE, 1)
    return (
        jnp.einsum("lgd,kd->glk", head_queries, head_keys, preferred_element_type=jnp.float32)
        * score_scale,
        head_keys,
    )


def attend(query_rows, key_rows, value_rows, allowed, score_scale):
    count_of_queries = query_rows.shape[0]
    kv_heads = key_rows.shape[1] // HEAD_SIZE
    query_groups = QUERY_HEADS // KEY_VALUE_HEADS
    group_width = query_groups * HEAD_SIZE

    def attend_one_head(head_index, loop_state):
        attn_out, log_totals = loop_state
        scores, head_keys = head_scores(query_rows, key_rows, head_index, score_scale)
        scores = jnp.where(allowed[None], scores, -jnp.inf)
        row_max = jnp.max(scores, axis=-1, keepdims=True)
        log_total = row_max[..., 0] + jnp.log(jnp.sum(jnp.exp(scores - row_max), axis=-1))
        rounded_length = jnp.exp(scores - log_total[..., None]).astype(jnp.bfloat16)
        head_values = lax.dynamic_slice_in_dim(value_rows, head_index * HEAD_SIZE, HEAD_SIZE, 1)
        head_out = jnp.einsum(
            "glk,kd->lgd", rounded_length, head_values, preferred_element_type=jnp.float32
        ).astype(jnp.bfloat16)
        attn_out = lax.dynamic_update_slice_in_dim(
            attn_out, head_out.reshape(count_of_queries, group_width), head_index * group_width, 1
        )
        log_totals = lax.dynamic_update_slice_in_dim(log_totals, log_total[None], head_index, 0)
        return (attn_out, log_totals)

    initial = (
        jnp.zeros((count_of_queries, kv_heads * group_width), jnp.bfloat16),
        jnp.zeros((kv_heads, query_groups, count_of_queries), jnp.float32),
    )
    return lax.fori_loop(0, kv_heads, attend_one_head, initial)


def backward(
    query_rows,
    key_rows,
    value_rows,
    allowed,
    log_totals,
    output_gradient,
    attention_out,
    score_scale,
):
    count_of_queries = query_rows.shape[0]
    key_count = key_rows.shape[0]
    kv_heads = key_rows.shape[1] // HEAD_SIZE
    query_groups = QUERY_HEADS // KEY_VALUE_HEADS
    group_width = query_groups * HEAD_SIZE

    def backward_one_head(head_index, loop_state):
        query_sums, value_sums = loop_state
        scores, head_keys = head_scores(query_rows, key_rows, head_index, score_scale)
        log_total = lax.dynamic_index_in_dim(log_totals, head_index, 0, keepdims=False)
        weights = jnp.exp(jnp.where(allowed[None], scores, -jnp.inf) - log_total[..., None])
        rounded_length = weights.astype(jnp.bfloat16)
        head_values = lax.dynamic_slice_in_dim(value_rows, head_index * HEAD_SIZE, HEAD_SIZE, 1)
        head_grads = lax.dynamic_slice_in_dim(
            output_gradient, head_index * group_width, group_width, 1
        ).reshape(count_of_queries, query_groups, HEAD_SIZE)
        head_outs = lax.dynamic_slice_in_dim(
            attention_out, head_index * group_width, group_width, 1
        ).reshape(count_of_queries, query_groups, HEAD_SIZE)
        row_delta = jnp.sum(head_grads.astype(jnp.float32) * head_outs.astype(jnp.float32), axis=-1)
        grad_weights = jnp.einsum(
            "lgd,kd->glk", head_grads, head_values, preferred_element_type=jnp.float32
        )
        grad_scores = (weights * (grad_weights - row_delta.T[:, :, None]) * score_scale).astype(
            jnp.bfloat16
        )
        query_part = jnp.einsum(
            "glk,kd->lgd", grad_scores, head_keys, preferred_element_type=jnp.float32
        ).reshape(count_of_queries, group_width)
        value_portion = jnp.einsum(
            "glk,lgd->kd", rounded_length, head_grads, preferred_element_type=jnp.float32
        )
        query_sums = lax.dynamic_update_slice_in_dim(
            query_sums, query_part, head_index * group_width, 1
        )
        value_sums = lax.dynamic_update_slice_in_dim(
            value_sums, value_portion, head_index * HEAD_SIZE, 1
        )
        return (query_sums, value_sums)

    initial = (
        jnp.zeros((count_of_queries, kv_heads * group_width), jnp.float32),
        jnp.zeros((key_count, kv_heads * HEAD_SIZE), jnp.float32),
    )
    return lax.fori_loop(0, kv_heads, backward_one_head, initial)


def per_device(
    hidden_states,
    query_base,
    key_base,
    frozen_value_rows,
    query_down,
    query_up,
    value_down,
    value_up_weight,
    positions,
    block_mask,
    output_gradient,
):
    count_of_queries = hidden_states.shape[0]
    key_extent = WINDOW // count_of_queries
    key_range_length = (key_extent + 1) * count_of_queries
    score_scale = (D // QUERY_HEADS) ** (-0.5)
    mask_height = count_of_queries // BLOCK
    device_index = lax.axis_index("ctx")
    leading_token = device_index * count_of_queries
    tokens_all = count_of_queries * lax.axis_size("ctx")
    query_sum, value_sum = lax.psum(
        (
            jnp.dot(hidden_states, query_down, preferred_element_type=jnp.float32),
            jnp.dot(hidden_states, value_down, preferred_element_type=jnp.float32),
        ),
        "head",
    )
    query_low = query_sum.astype(jnp.bfloat16)
    value_low = value_sum.astype(jnp.bfloat16)
    query_rows = rotate(
        query_base.astype(jnp.float32)
        + jnp.dot(query_low, query_up, preferred_element_type=jnp.float32),
        positions,
        1.0,
    ).astype(jnp.bfloat16)
    key_rows = rotate(key_base.astype(jnp.float32), positions, 1.0).astype(jnp.bfloat16)
    values = (
        frozen_value_rows.astype(jnp.float32)
        + jnp.dot(value_low, value_up_weight, preferred_element_type=jnp.float32)
    ).astype(jnp.bfloat16)
    earlier = []
    for distance in range(key_extent, 0, -1):
        earlier.append(shifted((key_rows, values), "ctx", distance))
    window_key_rows = jnp.concatenate([pair[0] for pair in earlier] + [key_rows], axis=0)
    window_value_rows = jnp.concatenate([pair[1] for pair in earlier] + [values], axis=0)
    own_mask = lax.dynamic_slice_in_dim(block_mask, device_index * mask_height, mask_height, 0)
    allowed = allowed_pairs(
        own_mask,
        leading_token,
        leading_token - key_extent * count_of_queries,
        count_of_queries,
        key_range_length,
    )
    attention_out, log_totals = attend(
        query_rows, window_key_rows, window_value_rows, allowed, score_scale
    )
    query_sums, value_sums = backward(
        query_rows,
        window_key_rows,
        window_value_rows,
        allowed,
        log_totals,
        output_gradient,
        attention_out,
        score_scale,
    )
    value_total = value_sums[key_extent * count_of_queries :]
    for distance in range(1, key_extent + 1):
        partial_value = value_sums[
            (key_extent - distance)
            * count_of_queries : (key_extent - distance + 1)
            * count_of_queries
        ]
        value_total = value_total + shifted(partial_value, "ctx", -distance)
    query_grad = rotate(query_sums, positions, -1.0).astype(jnp.bfloat16)
    value_grad = value_total.astype(jnp.bfloat16)
    contract_cols = (((1,), (1,)), ((), ()))
    contract_rows = (((0,), (0,)), ((), ()))
    query_part = lax.dot_general(
        query_grad, query_up, contract_cols, preferred_element_type=jnp.float32
    )
    value_portion = lax.dot_general(
        value_grad, value_up_weight, contract_cols, preferred_element_type=jnp.float32
    )
    query_back_sum, value_back_sum = lax.psum((query_part, value_portion), "head")
    query_back = query_back_sum.astype(jnp.bfloat16)
    value_back = value_back_sum.astype(jnp.bfloat16)
    down_query = lax.dot_general(
        query_back, hidden_states, contract_rows, preferred_element_type=jnp.float32
    )
    down_value = lax.dot_general(
        value_back, hidden_states, contract_rows, preferred_element_type=jnp.float32
    )
    up_query = lax.dot_general(
        query_low, query_grad, contract_rows, preferred_element_type=jnp.float32
    )
    up_value = lax.dot_general(
        value_low, value_grad, contract_rows, preferred_element_type=jnp.float32
    )
    loss_scale = tokens_all ** (-0.5)
    mine = (down_query, up_query, down_value, up_value)
    widths = tuple(part.shape[1] for part in mine)
    row = jnp.concatenate(mine, axis=1).astype(jnp.bfloat16)
    row = jnp.pad(row, ((0, 0), (0, GROUP * CHUNK - row.shape[1])))
    parts = row.reshape(RANK, GROUP, CHUNK).transpose(1, 0, 2)
    down_query, up_query, down_value, up_value = total_over_ctx(parts, widths, loss_scale)
    return attention_out, down_query.T, up_query, down_value.T, up_value


def solution(mesh):
    placed = (
        P("ctx", "head"),
        P("ctx", "head"),
        P("ctx", "head"),
        P("ctx", "head"),
        P("head", None),
        P(None, "head"),
        P("head", None),
        P(None, "head"),
        P("ctx"),
        P(),
        P("ctx", "head"),
    )
    return jax.shard_map(
        per_device,
        mesh=mesh,
        in_specs=placed,
        out_specs=(
            P("ctx", "head"),
            P("head", None),
            P(None, "head"),
            P("head", None),
            P(None, "head"),
        ),
        check_vma=False,
    )
```

```python
import functools
import math

import jax
import jax.numpy as jnp
import numpy as np
from jax import lax
from jax.experimental import pallas as pl
from jax.experimental.pallas import tpu as pltpu
from jax.sharding import PartitionSpec as P

D = 5376
QUERY_HEADS = 32
KEY_VALUE_HEADS = 16
HEAD_SIZE = 128
WINDOW = 1024
BLOCK = 128
ROPE_BASE = 10000.0

TOKENS = 512
FEATURES = 2688
KV = 8
PAIR = 2 * HEAD_SIZE
ROWS = 256
SPAN = WINDOW + ROWS
REACH = WINDOW + TOKENS
AHEAD = 3
LAG = 2
HIDDEN = -1e30
SCALE = (D // QUERY_HEADS) ** -0.5
BF16 = jnp.bfloat16
F32 = jnp.float32

RANK = 16
GROUP = 8
CHUNK = 1152
MESH = pl.DeviceIdType.MESH


def pieces_of(widths):
    pieces, start = [], 0
    for which, width in enumerate(widths):
        done = 0
        while done < width:
            chunk, inside = divmod(start + done, CHUNK)
            count = min(width - done, CHUNK - inside)
            pieces.append((which, done, chunk, inside, count))
            done += count
        start += width
    return pieces


def total_kernel(
    widths,
    scale,
    parts,
    o_0,
    o_1,
    o_2,
    o_3,
    near,
    far,
    final,
    near_send,
    near_recv,
    far_send,
    far_recv,
    final_send,
    final_recv,
):
    ctx, head = lax.axis_index("ctx"), lax.axis_index("head")
    member = ctx % GROUP
    group = ctx // GROUP
    near_peers = [group * GROUP + (member + by) % GROUP for by in range(1, GROUP)]
    far_peers = [((group + by) % GROUP) * GROUP + member for by in range(1, GROUP)]

    barrier = pltpu.get_barrier_semaphore()
    for peer in near_peers + far_peers:
        pl.semaphore_signal(barrier, inc=1, device_id=(peer, head), device_id_type=MESH)
    pl.semaphore_wait(barrier, 2 * (GROUP - 1))

    def copy(source, target, send, recv, peer):
        return pltpu.make_async_remote_copy(
            src_ref=source,
            dst_ref=target,
            send_sem=send,
            recv_sem=recv,
            device_id=(peer, head),
            device_id_type=MESH,
        )

    copies = []
    for k, peer in enumerate(near_peers):
        one = copy(
            parts.at[peer % GROUP], near.at[k], near_send.at[k], near_recv.at[k], peer
        )
        one.start()
        copies.append(one)
    total = parts[member].astype(jnp.float32)
    for k, one in enumerate(copies):
        one.wait_recv()
        total += near[k].astype(jnp.float32)
    far[group] = total.astype(jnp.bfloat16)

    far_copies = []
    for k, peer in enumerate(far_peers):
        one = copy(far.at[group], far.at[group], far_send.at[k], far_recv.at[k], peer)
        one.start()
        far_copies.append(one)
    for one in far_copies:
        one.wait_recv()
    total = far[0].astype(jnp.float32)
    for k in range(1, GROUP):
        total += far[k].astype(jnp.float32)
    final[member] = (total * scale).astype(jnp.bfloat16)

    last_copies = []
    for k, peer in enumerate(near_peers):
        one = copy(final.at[member], final.at[member], final_send.at[k], final_recv.at[k], peer)
        one.start()
        last_copies.append(one)
    for one in last_copies:
        one.wait_recv()
    outs = (o_0, o_1, o_2, o_3)
    for which, at, chunk, inside, count in pieces_of(widths):
        outs[which][:, at : at + count] = final[chunk, :, inside : inside + count].astype(
            jnp.float32
        )
    for one in copies + far_copies + last_copies:
        one.wait_send()


def total_over_ctx(parts, widths, scale):
    chunked = (GROUP, RANK, CHUNK)
    return pl.pallas_call(
        functools.partial(total_kernel, widths, scale),
        out_shape=[jax.ShapeDtypeStruct((RANK, width), jnp.float32) for width in widths],
        in_specs=[pl.BlockSpec(memory_space=pltpu.VMEM)],
        out_specs=[pl.BlockSpec(memory_space=pltpu.VMEM)] * len(widths),
        scratch_shapes=[
            pltpu.VMEM((GROUP - 1, RANK, CHUNK), jnp.bfloat16),
            pltpu.VMEM(chunked, jnp.bfloat16),
            pltpu.VMEM(chunked, jnp.bfloat16),
        ]
        + [pltpu.SemaphoreType.DMA((GROUP - 1,))] * 6,
        compiler_params=pltpu.CompilerParams(
            collective_id=0, has_side_effects=True, vmem_limit_bytes=24 * 2**20
        ),
    )(parts)


def turns_of_angles():
    half = HEAD_SIZE // 2
    turns = ROPE_BASE ** (-2.0 * np.arange(half) / HEAD_SIZE) / (2.0 * math.pi)
    mantissa, exponent = np.frexp(turns)
    coarse = np.ldexp(np.floor(mantissa * 256.0), exponent - 8)
    rows = np.stack([np.tile(coarse, 2), np.tile(turns - coarse, 2)])
    return np.concatenate([rows, np.zeros((6, HEAD_SIZE))]).astype(np.float32)


def nearest(x):
    return jnp.floor(x + 0.5)


def sine_of_turns(r):
    r = r - nearest(r)
    r = jnp.where(r > 0.25, 0.5 - r, jnp.where(r < -0.25, -0.5 - r, r))
    x = r * (2.0 * math.pi)
    y = x * x
    out = jnp.full_like(y, -1.0 / math.factorial(11))
    for power in (9, 7, 5, 3, 1):
        sign = 1.0 if power % 4 == 1 else -1.0
        out = out * y + sign / math.factorial(power)
    return out * x


def dot(a, b, contract):
    return lax.dot_general(a, b, ((contract[:1], contract[1:]), ((), ())), preferred_element_type=F32)


def layer_kernel(
    hidden_hbm,
    query_hbm,
    key_hbm,
    value_hbm,
    query_down_hbm,
    query_up_hbm,
    value_down_hbm,
    value_up_hbm,
    positions_ref,
    turns_ref,
    mask_ref,
    gradient_hbm,
    out_hbm,
    parts_ref,
    hidden,
    query_base,
    key_base,
    value_base,
    downs,
    query_up,
    value_up,
    gradient,
    keys,
    values,
    out,
    bias,
    cosines,
    sines,
    low_mine,
    low_theirs,
    low_rows,
    low_cols,
    back_mine,
    back_theirs,
    query_grad,
    value_sum,
    value_own,
    value_sent,
    value_got,
    row,
    load_sem,
    out_sem,
    low_sem,
    back_sem,
    far_send,
    far_recv,
    near_send,
    near_recv,
    grad_send,
    grad_recv,
):
    ctx, head = lax.axis_index("ctx"), lax.axis_index("head")
    count = lax.axis_size("ctx")
    core = ctx % 2
    ahead_1, ahead_2 = (ctx + 1) % count, (ctx + 2) % count
    behind_1, behind_2 = (ctx + count - 1) % count, (ctx + count - 2) % count

    def remote(source, target, send, recv, at_ctx, at_head=head):
        return pltpu.make_async_remote_copy(
            src_ref=source,
            dst_ref=target,
            send_sem=send,
            recv_sem=recv,
            device_id=(at_ctx, at_head),
            device_id_type=MESH,
        )

    loads = [
        pltpu.make_async_copy(source, target, load_sem.at[k])
        for k, (source, target) in enumerate(
            (
                (key_hbm, key_base),
                (query_down_hbm, downs.at[0:RANK]),
                (value_down_hbm, downs.at[RANK : 2 * RANK]),
                (hidden_hbm, hidden),
                (value_up_hbm, value_up.at[RANK : 2 * RANK]),
                (value_hbm, value_base),
                (query_up_hbm, query_up.at[0:RANK]),
                (query_hbm, query_base),
                (gradient_hbm, gradient),
            )
        )
    ]
    for one in loads:
        one.start()

    barrier = pltpu.get_barrier_semaphore()
    for at in ((ahead_1, head), (ahead_2, head), (behind_1, head), (behind_2, head), (ctx, 1 - head)):
        pl.semaphore_signal(barrier, inc=1, device_id=at, device_id_type=MESH)

    lane = lax.broadcasted_iota(jnp.int32, (TOKENS, HEAD_SIZE), 1)
    first_half = lane < HEAD_SIZE // 2
    position = jnp.transpose(
        jnp.broadcast_to(positions_ref[...].astype(F32), (HEAD_SIZE, TOKENS))
    )
    coarse = position * turns_ref[0:1, :]
    fine = position * turns_ref[1:2, :]
    turns = (coarse - nearest(coarse)) + (fine - nearest(fine))
    table = sine_of_turns(turns + jnp.where(first_half, 0.25, 0.0))
    swapped = pltpu.roll(table, HEAD_SIZE // 2, 1)
    cosines[...] = jnp.where(first_half, table, swapped)
    sines[...] = jnp.where(first_half, -swapped, table)

    def rope(x, cos, sin):
        return x * cos + pltpu.roll(x, HEAD_SIZE // 2, 1) * sin

    loads[0].wait()
    for h in range(KV):
        columns = slice(h * HEAD_SIZE, (h + 1) * HEAD_SIZE)
        keys[h, WINDOW:REACH] = rope(
            key_base[:, columns].astype(F32), cosines[...], sines[...]
        ).astype(BF16)

    pl.semaphore_wait(barrier, 5)

    def far_copy(store, kind, h):
        return remote(
            store.at[h, WINDOW:REACH],
            store.at[h, 0:TOKENS],
            far_send.at[kind, h],
            far_recv.at[kind, h],
            ahead_2,
        )

    def near_copy(store, kind, h, first, at_ctx):
        return remote(
            store.at[h, pl.ds(first, TOKENS)],
            store.at[h, TOKENS:WINDOW],
            near_send.at[kind, h],
            near_recv.at[kind, h],
            at_ctx,
        )

    def send_own(store, kind, h):
        far_copy(store, kind, h).start()

        @pl.when(core == 0)
        def _():
            near_copy(store, kind, h, WINDOW, ahead_1).start()

    for h in range(AHEAD):
        send_own(keys, 0, h)

    for one in loads[1:4]:
        one.wait()
    low_mine[...] = dot(downs[...], hidden[...], (1, 1))
    low_copy = remote(low_mine, low_theirs, low_sem.at[0], low_sem.at[1], ctx, 1 - head)
    low_copy.start()

    key_at = lax.broadcasted_iota(jnp.int32, (BLOCK, BLOCK), 1)
    query_at = lax.broadcasted_iota(jnp.int32, (BLOCK, BLOCK), 0)
    for half in range(TOKENS // ROWS):
        for r in range(ROWS // BLOCK):
            block = ctx * (TOKENS // BLOCK) + half * (ROWS // BLOCK) + r
            for j in range(SPAN // BLOCK):
                offset = WINDOW // BLOCK + r - j
                if 0 <= offset <= WINDOW // BLOCK:
                    seen = (mask_ref[offset, block] == 1) & (block >= offset)
                    tile = jnp.full((BLOCK, BLOCK), jnp.where(seen, 0.0, HIDDEN))
                    if offset == 0:
                        tile = jnp.where(key_at <= query_at, tile, HIDDEN)
                    if offset == WINDOW // BLOCK:
                        tile = jnp.where(key_at > query_at, tile, HIDDEN)
                else:
                    tile = jnp.full((BLOCK, BLOCK), HIDDEN, F32)
                bias[
                    half, r * BLOCK : (r + 1) * BLOCK, j * BLOCK : (j + 1) * BLOCK
                ] = tile

    query_up[RANK : 2 * RANK] = jnp.zeros((RANK, KV * PAIR), BF16)
    value_up[0:RANK] = jnp.zeros((RANK, KV * HEAD_SIZE), BF16)
    back_mine[...] = jnp.zeros_like(back_mine)
    row[...] = jnp.zeros_like(row)

    low_copy.wait_recv()
    low = low_mine[...] + low_theirs[...]
    low_rows[...] = low.astype(BF16)
    low_cols[...] = jnp.transpose(low).astype(BF16)
    loads[4].wait()
    loads[5].wait()
    for h in range(KV):
        columns = slice(h * HEAD_SIZE, (h + 1) * HEAD_SIZE)
        values[h, WINDOW:REACH] = (
            value_base[:, columns].astype(F32) + dot(low_cols[...], value_up[:, columns], (1, 0))
        ).astype(BF16)
        if h < AHEAD:
            send_own(values, 1, h)
    for one in loads[6:]:
        one.wait()

    widths = (FEATURES, KV * PAIR, FEATURES, KV * HEAD_SIZE)

    def out_copy(h):
        columns = pl.ds(pl.multiple_of(h * PAIR, PAIR), PAIR)
        return pltpu.make_async_copy(out.at[:, columns], out_hbm.at[:, columns], out_sem.at[h])

    def grad_copy(kind, h):
        return remote(
            value_sent.at[h, kind],
            value_got.at[h, kind],
            grad_send.at[kind, h],
            grad_recv.at[kind, h],
            behind_1 if kind == 0 else behind_2,
        )

    def half_of(h, half):
        rows = slice(half * ROWS, (half + 1) * ROWS)
        span = slice(half * ROWS, half * ROWS + SPAN)
        pair = pl.ds(pl.multiple_of(h * PAIR, PAIR), PAIR)
        cos, sin = cosines[rows], sines[rows]

        def stack(x):
            return jnp.concatenate([x[:, :HEAD_SIZE], x[:, HEAD_SIZE:]], axis=0)

        cos_2 = jnp.concatenate([cos, cos], axis=0)
        sin_2 = jnp.concatenate([sin, sin], axis=0)
        raw = query_base[rows, pair].astype(F32) + dot(
            low_cols[rows], query_up[:, pair], (1, 0)
        )
        queries = (rope(stack(raw), cos_2, sin_2) * (SCALE * math.log2(math.e))).astype(BF16)
        head_keys, head_values = keys[h, span], values[h, span]
        scores = dot(queries, head_keys, (1, 1))
        scores = (
            scores.reshape(2, ROWS, SPAN) + bias[half][None]
        ).reshape(2 * ROWS, SPAN)
        top = jnp.max(scores, axis=1, keepdims=True)
        weights = jnp.exp2(scores - top)
        inverse = 1.0 / jnp.sum(weights, axis=1, keepdims=True)
        rounded = weights.astype(BF16)
        result = (dot(rounded, head_values, (1, 0)) * inverse).astype(BF16)
        out[rows, pair] = jnp.concatenate([result[:ROWS], result[ROWS:]], axis=1)
        scaled = stack(gradient[rows, pair]).astype(F32) * inverse
        delta = jnp.sum(scaled * result.astype(F32), axis=1, keepdims=True)
        scaled = scaled.astype(BF16)
        grad_weights = dot(scaled, head_values, (1, 1))
        grad_scores = (weights * (grad_weights - delta)).astype(BF16)
        turned = rope(dot(grad_scores, head_keys, (1, 0)) * SCALE, cos_2, -sin_2).astype(BF16)
        query_grad[rows] = jnp.concatenate([turned[:ROWS], turned[ROWS:]], axis=1)
        terms = dot(scaled, rounded, (0, 0))
        if half == 0:
            value_sum[:, 0:SPAN] = terms
        else:
            value_sum[:, ROWS:SPAN] += terms[:, : SPAN - ROWS]
            value_sum[:, SPAN:REACH] = terms[:, SPAN - ROWS :]

    def absorb(h):
        grad_copy(0, h).wait_recv()
        grad_copy(1, h).wait_recv()
        total = (
            value_own[h] + value_got[h, 0].astype(F32) + value_got[h, 1].astype(F32)
        ).astype(BF16)
        columns = pl.ds(pl.multiple_of(h * HEAD_SIZE, HEAD_SIZE), HEAD_SIZE)
        back_mine[RANK : 2 * RANK] += dot(value_up[RANK : 2 * RANK, columns], total, (1, 0))
        row[:, pl.ds(pl.multiple_of(h * HEAD_SIZE, HEAD_SIZE) + sum(widths[:3]), HEAD_SIZE)] = dot(
            low_rows[RANK : 2 * RANK], total, (1, 1)
        )

    def one_head(h, carry):
        far_copy(keys, 0, h).wait_recv()
        far_copy(values, 1, h).wait_recv()

        @pl.when(core == 1)
        def _():
            near_copy(keys, 0, h, 0, behind_1).start()
            near_copy(values, 1, h, 0, behind_1).start()

        @pl.when(h + AHEAD < KV)
        def _():
            send_own(keys, 0, h + AHEAD)
            send_own(values, 1, h + AHEAD)

        near_copy(keys, 0, h, 0, behind_1).wait_recv()
        near_copy(values, 1, h, 0, behind_1).wait_recv()
        half_of(h, 0)
        half_of(h, 1)
        value_sent[h, 1] = value_sum[:, 0:TOKENS].astype(BF16)
        value_sent[h, 0] = value_sum[:, TOKENS:WINDOW].astype(BF16)
        grad_copy(1, h).start()
        grad_copy(0, h).start()
        value_own[h] = value_sum[:, WINDOW:REACH]
        out_copy(h).start()
        pair = pl.ds(pl.multiple_of(h * PAIR, PAIR), PAIR)
        back_mine[0:RANK] += dot(query_up[0:RANK, pair], query_grad[...], (1, 1))
        row[:, pl.ds(pl.multiple_of(h * PAIR, PAIR) + widths[0], PAIR)] = dot(
            low_rows[0:RANK], query_grad[...], (1, 0)
        )

        @pl.when(h >= LAG)
        def _():
            absorb(h - LAG)

        return carry

    lax.fori_loop(0, KV, one_head, 0)
    for h in range(KV - LAG, KV):
        absorb(h)

    back_copy = remote(back_mine, back_theirs, back_sem.at[0], back_sem.at[1], ctx, 1 - head)
    back_copy.start()
    back_copy.wait_recv()
    back = (back_mine[...] + back_theirs[...]).astype(BF16)
    down = dot(back, hidden[...], (1, 0))
    row[:, 0:FEATURES] = down[0:RANK]
    start = widths[0] + widths[1]
    row[:, start : start + FEATURES] = down[RANK:]
    for k in range(GROUP):
        parts_ref[k] = row[:, k * CHUNK : (k + 1) * CHUNK].astype(BF16)

    low_copy.wait_send()
    back_copy.wait_send()

    def finish(h, carry):
        for kind, store in ((0, keys), (1, values)):
            far_copy(store, kind, h).wait_send()
            near_copy(store, kind, h, 0, behind_1).wait_send()
            grad_copy(kind, h).wait_send()
        out_copy(h).wait()
        return carry

    lax.fori_loop(0, KV, finish, 0)


def per_device(
    hidden_states,
    query_base,
    key_base,
    frozen_value_rows,
    query_down,
    query_up,
    value_down,
    value_up_weight,
    positions,
    block_mask,
    output_gradient,
):
    anywhere = pl.BlockSpec(memory_space=pl.ANY)
    in_vmem = pl.BlockSpec(memory_space=pltpu.VMEM)
    columns = KV * HEAD_SIZE
    head_store = pltpu.VMEM((KV, REACH, HEAD_SIZE), BF16)
    value_terms = pltpu.VMEM((KV, 2, HEAD_SIZE, TOKENS), BF16)
    low_shape = pltpu.VMEM((2 * RANK, TOKENS), F32)
    dma = pltpu.SemaphoreType.DMA
    attention_out, parts = pl.pallas_call(
        layer_kernel,
        out_shape=[
            jax.ShapeDtypeStruct((TOKENS, 2 * columns), BF16),
            jax.ShapeDtypeStruct((GROUP, RANK, CHUNK), BF16),
        ],
        in_specs=[anywhere] * 8
        + [in_vmem, in_vmem, pl.BlockSpec(memory_space=pltpu.SMEM), anywhere],
        out_specs=[anywhere, in_vmem],
        scratch_shapes=[
            pltpu.VMEM((TOKENS, FEATURES), BF16),
            pltpu.VMEM((TOKENS, 2 * columns), BF16),
            pltpu.VMEM((TOKENS, columns), BF16),
            pltpu.VMEM((TOKENS, columns), BF16),
            pltpu.VMEM((2 * RANK, FEATURES), BF16),
            pltpu.VMEM((2 * RANK, 2 * columns), BF16),
            pltpu.VMEM((2 * RANK, columns), BF16),
            pltpu.VMEM((TOKENS, 2 * columns), BF16),
            head_store,
            head_store,
            pltpu.VMEM((TOKENS, 2 * columns), BF16),
            pltpu.VMEM((TOKENS // ROWS, ROWS, SPAN), F32),
            pltpu.VMEM((TOKENS, HEAD_SIZE), F32),
            pltpu.VMEM((TOKENS, HEAD_SIZE), F32),
            low_shape,
            low_shape,
            pltpu.VMEM((2 * RANK, TOKENS), BF16),
            pltpu.VMEM((TOKENS, 2 * RANK), BF16),
            low_shape,
            low_shape,
            pltpu.VMEM((TOKENS, PAIR), BF16),
            pltpu.VMEM((HEAD_SIZE, REACH), F32),
            pltpu.VMEM((KV, HEAD_SIZE, TOKENS), F32),
            value_terms,
            value_terms,
            pltpu.VMEM((RANK, GROUP * CHUNK), F32),
            dma((9,)),
            dma((KV,)),
            dma((2,)),
            dma((2,)),
        ]
        + [dma((2, KV))] * 6,
        compiler_params=pltpu.CompilerParams(
            collective_id=1, has_side_effects=True, vmem_limit_bytes=56 * 2**20
        ),
    )(
        hidden_states,
        query_base,
        key_base,
        frozen_value_rows,
        query_down.T,
        query_up,
        value_down.T,
        value_up_weight,
        positions.reshape(1, TOKENS),
        turns_of_angles(),
        block_mask.T,
        output_gradient,
    )
    widths = (FEATURES, 2 * columns, FEATURES, columns)
    tokens_all = TOKENS * lax.axis_size("ctx")
    down_query, up_query, down_value, up_value = total_over_ctx(
        parts, widths, tokens_all**-0.5
    )
    return attention_out, down_query.T, up_query, down_value.T, up_value


def solution(mesh):
    placed = (
        P("ctx", "head"),
        P("ctx", "head"),
        P("ctx", "head"),
        P("ctx", "head"),
        P("head", None),
        P(None, "head"),
        P("head", None),
        P(None, "head"),
        P("ctx"),
        P(),
        P("ctx", "head"),
    )
    return jax.shard_map(
        per_device,
        mesh=mesh,
        in_specs=placed,
        out_specs=(
            P("ctx", "head"),
            P("head", None),
            P(None, "head"),
            P("head", None),
            P(None, "head"),
        ),
        check_vma=False,
    )
```

```python
import functools
import math

import jax
import jax.numpy as jnp
import numpy as np
from jax import lax
from jax.experimental import pallas as pl
from jax.experimental.pallas import tpu as pltpu
from jax.sharding import PartitionSpec as P

D = 5376
QUERY_HEADS = 32
KEY_VALUE_HEADS = 16
HEAD_SIZE = 128
WINDOW = 1024
BLOCK = 128
ROPE_BASE = 10000.0

TOKENS = 512
FEATURES = 2688
KV = 8
PAIR = 2 * HEAD_SIZE
ROWS = 256
SPAN = WINDOW + ROWS
REACH = WINDOW + TOKENS
AHEAD = 4
LAG = 3
HIDDEN = -1e30
SCALE = (D // QUERY_HEADS) ** -0.5
BF16 = jnp.bfloat16
F32 = jnp.float32

RANK = 16
GROUP = 8
PIECES = 4
MESH = pl.DeviceIdType.MESH


def pieces_of(widths, chunk_width):
    pieces, start = [], 0
    for which, width in enumerate(widths):
        done = 0
        while done < width:
            chunk, inside = divmod(start + done, chunk_width)
            size = min(width - done, chunk_width - inside)
            pieces.append((which, done, chunk, inside, size))
            done += size
        start += width
    return pieces


def turns_of_angles():
    half = HEAD_SIZE // 2
    turns = ROPE_BASE ** (-2.0 * np.arange(half) / HEAD_SIZE) / (2.0 * math.pi)
    mantissa, exponent = np.frexp(turns)
    coarse = np.ldexp(np.floor(mantissa * 256.0), exponent - 8)
    rows = np.stack([np.tile(coarse, 2), np.tile(turns - coarse, 2)])
    return np.concatenate([rows, np.zeros((6, HEAD_SIZE))]).astype(np.float32)


def nearest(x):
    return jnp.floor(x + 0.5)


def sine_of_turns(r):
    r = r - nearest(r)
    r = jnp.where(r > 0.25, 0.5 - r, jnp.where(r < -0.25, -0.5 - r, r))
    x = r * (2.0 * math.pi)
    y = x * x
    out = jnp.full_like(y, -1.0 / math.factorial(11))
    for power in (9, 7, 5, 3, 1):
        sign = 1.0 if power % 4 == 1 else -1.0
        out = out * y + sign / math.factorial(power)
    return out * x


def dot(a, b, contract):
    return lax.dot_general(a, b, ((contract[:1], contract[1:]), ((), ())), preferred_element_type=F32)


def layer_kernel(
    hidden_hbm,
    query_hbm,
    key_hbm,
    value_hbm,
    query_down_hbm,
    query_up_hbm,
    value_down_hbm,
    value_up_hbm,
    positions_ref,
    turns_ref,
    mask_ref,
    gradient_hbm,
    out_hbm,
    final_query,
    final_value,
    hidden,
    query_base,
    key_base,
    value_base,
    downs,
    query_up,
    value_up,
    gradient,
    keys,
    values,
    out,
    bias,
    cosines,
    sines,
    low_mine,
    low_theirs,
    low_rows,
    low_cols,
    back_mine,
    back_theirs,
    query_grad,
    value_sum,
    value_own,
    value_sent,
    value_got,
    row_query,
    row_value,
    parts_query,
    parts_value,
    near_query,
    near_value,
    away_query,
    away_value,
    load_sem,
    out_sem,
    low_sem,
    back_sem,
    far_send,
    far_recv,
    near_send,
    near_recv,
    grad_send,
    grad_recv,
    sum_send,
    sum_recv,
):
    ctx, head = lax.axis_index("ctx"), lax.axis_index("head")
    count = lax.axis_size("ctx")
    core = ctx % 2
    ahead_1, ahead_2 = (ctx + 1) % count, (ctx + 2) % count
    behind_1, behind_2 = (ctx + count - 1) % count, (ctx + count - 2) % count

    def remote(source, target, send, recv, at_ctx, at_head=head):
        return pltpu.make_async_remote_copy(
            src_ref=source,
            dst_ref=target,
            send_sem=send,
            recv_sem=recv,
            device_id=(at_ctx, at_head),
            device_id_type=MESH,
        )

    loads = [
        pltpu.make_async_copy(source, target, load_sem.at[k])
        for k, (source, target) in enumerate(
            (
                (key_hbm, key_base),
                (query_down_hbm, downs.at[0:RANK]),
                (value_down_hbm, downs.at[RANK : 2 * RANK]),
                (hidden_hbm, hidden),
                (value_up_hbm, value_up.at[RANK : 2 * RANK]),
                (value_hbm, value_base),
                (query_up_hbm, query_up.at[0:RANK]),
                (query_hbm, query_base),
                (gradient_hbm, gradient),
            )
        )
    ]
    for one in loads:
        one.start()

    barrier = pltpu.get_barrier_semaphore()
    member, group = ctx % GROUP, ctx // GROUP
    groups = count // GROUP
    near_peers = [group * GROUP + (member + by) % GROUP for by in range(1, GROUP)]
    far_peers = [((group + by) % groups) * GROUP + member for by in range(1, groups)]
    greeted = [(at, head) for at in (ahead_1, ahead_2, behind_1, behind_2)]
    greeted += [(ctx, 1 - head)] + [(at, head) for at in near_peers + far_peers]
    for at in greeted:
        pl.semaphore_signal(barrier, inc=1, device_id=at, device_id_type=MESH)

    lane = lax.broadcasted_iota(jnp.int32, (TOKENS, HEAD_SIZE), 1)
    first_half = lane < HEAD_SIZE // 2
    position = jnp.transpose(
        jnp.broadcast_to(positions_ref[...].astype(F32), (HEAD_SIZE, TOKENS))
    )
    coarse = position * turns_ref[0:1, :]
    fine = position * turns_ref[1:2, :]
    turns = (coarse - nearest(coarse)) + (fine - nearest(fine))
    table = sine_of_turns(turns + jnp.where(first_half, 0.25, 0.0))
    swapped = pltpu.roll(table, HEAD_SIZE // 2, 1)
    cosines[...] = jnp.where(first_half, table, swapped)
    sines[...] = jnp.where(first_half, -swapped, table)

    def rope(x, cos, sin):
        return x * cos + pltpu.roll(x, HEAD_SIZE // 2, 1) * sin

    loads[0].wait()
    for h in range(KV):
        columns = slice(h * HEAD_SIZE, (h + 1) * HEAD_SIZE)
        keys[h, WINDOW:REACH] = rope(
            key_base[:, columns].astype(F32), cosines[...], sines[...]
        ).astype(BF16)

    pl.semaphore_wait(barrier, len(greeted))

    def far_copy(store, kind, h):
        return remote(
            store.at[h, WINDOW:REACH],
            store.at[h, 0:TOKENS],
            far_send.at[kind, h],
            far_recv.at[kind, h],
            ahead_2,
        )

    def near_copy(store, kind, h, first, at_ctx):
        return remote(
            store.at[h, pl.ds(first, TOKENS)],
            store.at[h, TOKENS:WINDOW],
            near_send.at[kind, h],
            near_recv.at[kind, h],
            at_ctx,
        )

    def send_own(store, kind, h):
        @pl.when(ctx + 2 < count)
        def _():
            far_copy(store, kind, h).start()

        @pl.when(core == 0)
        def _():
            near_copy(store, kind, h, WINDOW, ahead_1).start()

    for h in range(AHEAD):
        send_own(keys, 0, h)

    for one in loads[1:4]:
        one.wait()
    low_mine[...] = dot(downs[...], hidden[...], (1, 1))
    low_copy = remote(low_mine, low_theirs, low_sem.at[0], low_sem.at[1], ctx, 1 - head)
    low_copy.start()

    key_at = lax.broadcasted_iota(jnp.int32, (BLOCK, BLOCK), 1)
    query_at = lax.broadcasted_iota(jnp.int32, (BLOCK, BLOCK), 0)
    for half in range(TOKENS // ROWS):
        for r in range(ROWS // BLOCK):
            block = ctx * (TOKENS // BLOCK) + half * (ROWS // BLOCK) + r
            for j in range(SPAN // BLOCK):
                offset = WINDOW // BLOCK + r - j
                if 0 <= offset <= WINDOW // BLOCK:
                    seen = (mask_ref[offset, block] == 1) & (block >= offset)
                    tile = jnp.full((BLOCK, BLOCK), jnp.where(seen, 0.0, HIDDEN))
                    if offset == 0:
                        tile = jnp.where(key_at <= query_at, tile, HIDDEN)
                    if offset == WINDOW // BLOCK:
                        tile = jnp.where(key_at > query_at, tile, HIDDEN)
                else:
                    tile = jnp.full((BLOCK, BLOCK), HIDDEN, F32)
                bias[
                    half, r * BLOCK : (r + 1) * BLOCK, j * BLOCK : (j + 1) * BLOCK
                ] = tile

    query_up[RANK : 2 * RANK] = jnp.zeros((RANK, KV * PAIR), BF16)
    value_up[0:RANK] = jnp.zeros((RANK, KV * HEAD_SIZE), BF16)
    back_mine[...] = jnp.zeros_like(back_mine)
    for padded, used in ((row_query, FEATURES + KV * PAIR), (row_value, FEATURES + KV * HEAD_SIZE)):
        padded[:, used:] = jnp.zeros((RANK, padded.shape[1] - used), F32)

    @pl.when(ctx < 2)
    def _():
        for store in (keys, values):
            store[:, 0:TOKENS] = jnp.zeros((KV, TOKENS, HEAD_SIZE), BF16)

    @pl.when(ctx < 1)
    def _():
        for store in (keys, values):
            store[:, TOKENS:WINDOW] = jnp.zeros((KV, TOKENS, HEAD_SIZE), BF16)

    @pl.when(ctx + 2 >= count)
    def _():
        value_got[:, 1] = jnp.zeros((KV, HEAD_SIZE, TOKENS), BF16)

    @pl.when(ctx + 1 >= count)
    def _():
        value_got[:, 0] = jnp.zeros((KV, HEAD_SIZE, TOKENS), BF16)

    low_copy.wait_recv()
    low = low_mine[...] + low_theirs[...]
    low_rows[...] = low.astype(BF16)
    low_cols[...] = jnp.transpose(low).astype(BF16)
    loads[4].wait()
    loads[5].wait()
    for h in range(KV):
        columns = slice(h * HEAD_SIZE, (h + 1) * HEAD_SIZE)
        values[h, WINDOW:REACH] = (
            value_base[:, columns].astype(F32) + dot(low_cols[...], value_up[:, columns], (1, 0))
        ).astype(BF16)
        if h < AHEAD:
            send_own(values, 1, h)
    for one in loads[6:]:
        one.wait()

    def out_copy(h):
        columns = pl.ds(pl.multiple_of(h * PAIR, PAIR), PAIR)
        return pltpu.make_async_copy(out.at[:, columns], out_hbm.at[:, columns], out_sem.at[h])

    def grad_copy(kind, h):
        return remote(
            value_sent.at[h, kind],
            value_got.at[h, kind],
            grad_send.at[kind, h],
            grad_recv.at[kind, h],
            behind_1 if kind == 0 else behind_2,
        )

    def stack(x):
        return jnp.concatenate([x[:, :HEAD_SIZE], x[:, HEAD_SIZE:]], axis=0)

    def beside(x):
        return jnp.concatenate([x[:ROWS], x[ROWS:]], axis=1)

    def both_halves(h):
        pair = pl.ds(pl.multiple_of(h * PAIR, PAIR), PAIR)
        halves = range(TOKENS // ROWS)
        rows = [slice(half * ROWS, (half + 1) * ROWS) for half in halves]
        span = [slice(half * ROWS, half * ROWS + SPAN) for half in halves]
        cos = [jnp.concatenate([cosines[rows[half]]] * 2, axis=0) for half in halves]
        sin = [jnp.concatenate([sines[rows[half]]] * 2, axis=0) for half in halves]

        def score(half):
            raw = query_base[rows[half], pair].astype(F32) + dot(
                low_cols[rows[half]], query_up[:, pair], (1, 0)
            )
            queries = rope(stack(raw), cos[half], sin[half]) * (SCALE * math.log2(math.e))
            return dot(queries.astype(BF16), keys[h, span[half]], (1, 1))

        def attend(half, scores):
            scores = (
                scores.reshape(2, ROWS, SPAN) + bias[half][None]
            ).reshape(2 * ROWS, SPAN)
            weights = jnp.exp2(scores - jnp.max(scores, axis=1, keepdims=True))
            inverse = 1.0 / jnp.sum(weights, axis=1, keepdims=True)
            weights = weights.astype(BF16)
            result = (dot(weights, values[h, span[half]], (1, 0)) * inverse).astype(BF16)
            out[rows[half], pair] = beside(result)
            return weights, inverse, result

        def back(half, weights, inverse, result):
            out_grad = stack(gradient[rows[half], pair])
            grad_weights = dot(out_grad, values[h, span[half]], (1, 1))
            out_grad = out_grad.astype(F32)
            delta = jnp.sum(out_grad * result.astype(F32), axis=1, keepdims=True)
            terms = dot((out_grad * inverse).astype(BF16), weights, (0, 0))
            if half == 0:
                value_sum[:, 0:SPAN] = terms
            else:
                value_sum[:, ROWS:SPAN] += terms[:, : SPAN - ROWS]
                value_sum[:, SPAN:REACH] = terms[:, SPAN - ROWS :]
            grad_scores = weights * (grad_weights - delta).astype(BF16)
            turned = rope(
                dot(grad_scores, keys[h, span[half]], (1, 0)) * (inverse * SCALE),
                cos[half],
                -sin[half],
            )
            query_grad[rows[half]] = beside(turned.astype(BF16))

        scores = [score(half) for half in halves]
        attended = [attend(half, scores[half]) for half in halves]
        for half in halves:
            back(half, *attended[half])

    def absorb(h):
        @pl.when(ctx + 1 < count)
        def _():
            grad_copy(0, h).wait_recv()

        @pl.when(ctx + 2 < count)
        def _():
            grad_copy(1, h).wait_recv()

        total = (
            value_own[h] + value_got[h, 0].astype(F32) + value_got[h, 1].astype(F32)
        ).astype(BF16)
        columns = pl.ds(pl.multiple_of(h * HEAD_SIZE, HEAD_SIZE), HEAD_SIZE)
        back_mine[RANK : 2 * RANK] += dot(value_up[RANK : 2 * RANK, columns], total, (1, 0))
        row_value[:, pl.ds(pl.multiple_of(h * HEAD_SIZE, HEAD_SIZE) + FEATURES, HEAD_SIZE)] = dot(
            low_rows[RANK : 2 * RANK], total, (1, 1)
        )

    def one_head(h, carry):
        @pl.when(ctx >= 2)
        def _():
            far_copy(keys, 0, h).wait_recv()
            far_copy(values, 1, h).wait_recv()

        @pl.when((core == 1) & (ctx >= 2))
        def _():
            near_copy(keys, 0, h, 0, behind_1).start()
            near_copy(values, 1, h, 0, behind_1).start()

        @pl.when(h + AHEAD < KV)
        def _():
            send_own(keys, 0, h + AHEAD)
            send_own(values, 1, h + AHEAD)

        @pl.when(ctx >= 1)
        def _():
            near_copy(keys, 0, h, 0, behind_1).wait_recv()
            near_copy(values, 1, h, 0, behind_1).wait_recv()

        both_halves(h)
        value_sent[h, 1] = value_sum[:, 0:TOKENS].astype(BF16)
        value_sent[h, 0] = value_sum[:, TOKENS:WINDOW].astype(BF16)

        @pl.when(ctx >= 2)
        def _():
            grad_copy(1, h).start()

        @pl.when(ctx >= 1)
        def _():
            grad_copy(0, h).start()

        value_own[h] = value_sum[:, WINDOW:REACH]
        out_copy(h).start()
        pair = pl.ds(pl.multiple_of(h * PAIR, PAIR), PAIR)
        back_mine[0:RANK] += dot(query_up[0:RANK, pair], query_grad[...], (1, 1))
        row_query[:, pl.ds(pl.multiple_of(h * PAIR, HEAD_SIZE) + FEATURES, PAIR)] = dot(
            low_rows[0:RANK], query_grad[...], (1, 0)
        )

        @pl.when(h >= LAG)
        def _():
            absorb(h - LAG)

        return carry

    lax.fori_loop(0, KV, one_head, 0)

    def back_copy(kind):
        rows = pl.ds(kind * RANK, RANK)
        return remote(
            back_mine.at[rows],
            back_theirs.at[rows],
            back_sem.at[0, kind],
            back_sem.at[1, kind],
            ctx,
            1 - head,
        )

    stores = (
        (row_query, parts_query, near_query, away_query, final_query),
        (row_value, parts_value, near_value, away_value, final_value),
    )

    def sum_copy(kind, step, k, peer):
        _, parts, near, away, final = stores[kind]
        source, target = (
            (parts.at[peer % GROUP], near.at[k]),
            (away.at[group], away.at[group]),
            (final.at[member], final.at[member]),
        )[step]
        return remote(
            source, target, sum_send.at[kind, step, k], sum_recv.at[kind, step, k], peer
        )

    def sum_copies(kind, step):
        peers = far_peers if step == 1 else near_peers
        return [sum_copy(kind, step, k, peer) for k, peer in enumerate(peers)]

    def scatter(kind):
        row, parts = stores[kind][:2]
        rows = slice(kind * RANK, (kind + 1) * RANK)
        back_copy(kind).wait_recv()
        total = (back_mine[rows] + back_theirs[rows]).astype(BF16)
        row[:, 0:FEATURES] = dot(total, hidden[...], (1, 0))
        width = parts.shape[2]
        for k in range(GROUP):
            parts[k] = row[:, k * width : (k + 1) * width].astype(BF16)
        for one in sum_copies(kind, 0):
            one.start()

    def exchange(kind):
        _, parts, near, away, _ = stores[kind]
        total = parts[member].astype(F32)
        for k, one in enumerate(sum_copies(kind, 0)):
            one.wait_recv()
            total += near[k].astype(F32)
        away[group] = total.astype(BF16)
        for one in sum_copies(kind, 1):
            one.start()

    def gather(kind):
        away, final = stores[kind][3:]
        for one in sum_copies(kind, 1):
            one.wait_recv()
        total = away[0].astype(F32)
        for k in range(1, groups):
            total += away[k].astype(F32)
        final[member] = (total * (TOKENS * count) ** -0.5).astype(BF16)
        for one in sum_copies(kind, 2):
            one.start()

    back_copy(0).start()
    for h in range(KV - LAG, KV - 1):
        absorb(h)
    scatter(0)
    absorb(KV - 1)
    back_copy(1).start()
    exchange(0)
    scatter(1)
    gather(0)
    exchange(1)
    gather(1)
    low_copy.wait_send()
    for kind in range(2):
        for one in sum_copies(kind, 2):
            one.wait_recv()
        for step in range(3):
            for one in sum_copies(kind, step):
                one.wait_send()
        back_copy(kind).wait_send()

    def finish(h, carry):
        @pl.when(ctx + 2 < count)
        def _():
            far_copy(keys, 0, h).wait_send()
            far_copy(values, 1, h).wait_send()

        @pl.when((core == 0) | (ctx >= 2))
        def _():
            near_copy(keys, 0, h, 0, behind_1).wait_send()
            near_copy(values, 1, h, 0, behind_1).wait_send()

        @pl.when(ctx >= 1)
        def _():
            grad_copy(0, h).wait_send()

        @pl.when(ctx >= 2)
        def _():
            grad_copy(1, h).wait_send()

        out_copy(h).wait()
        return carry

    lax.fori_loop(0, KV, finish, 0)


def output_kernel(
    passed,
    final_query,
    final_value,
    attention_out,
    down_query,
    up_query,
    down_value,
    up_value,
    held,
    sem,
):
    size = TOKENS // PIECES

    def copy(k, step):
        piece = pl.ds(k * size, size)
        source, target = ((passed, held), (held, attention_out))[step]
        return pltpu.make_async_copy(source.at[piece], target.at[piece], sem.at[step, k])

    for k in range(PIECES):
        copy(k, 0).start()
    for k in range(PIECES):
        copy(k, 0).wait()
        copy(k, 1).start()
    for final, outs in ((final_query, (down_query, up_query)), (final_value, (down_value, up_value))):
        width = final.shape[2]
        for which, at, chunk, inside, size in pieces_of([o.shape[1] for o in outs], width):
            outs[which][:, at : at + size] = final[chunk, :, inside : inside + size].astype(F32)
    for k in range(PIECES):
        copy(k, 1).wait()


def per_device(
    hidden_states,
    query_base,
    key_base,
    frozen_value_rows,
    query_down,
    query_up,
    value_down,
    value_up_weight,
    positions,
    block_mask,
    output_gradient,
):
    anywhere = pl.BlockSpec(memory_space=pl.ANY)
    in_vmem = pl.BlockSpec(memory_space=pltpu.VMEM)
    columns = KV * HEAD_SIZE
    head_store = pltpu.VMEM((KV, REACH, HEAD_SIZE), BF16)
    value_terms = pltpu.VMEM((KV, 2, HEAD_SIZE, TOKENS), BF16)
    low_shape = pltpu.VMEM((2 * RANK, TOKENS), F32)
    query_sum = (GROUP, RANK, 5 * HEAD_SIZE)
    value_sum = (GROUP, RANK, 4 * HEAD_SIZE)
    dma = pltpu.SemaphoreType.DMA
    passed, final_query, final_value = pl.pallas_call(
        layer_kernel,
        out_shape=[
            jax.ShapeDtypeStruct((TOKENS, 2 * columns), BF16),
            jax.ShapeDtypeStruct(query_sum, BF16),
            jax.ShapeDtypeStruct(value_sum, BF16),
        ],
        in_specs=[anywhere] * 8
        + [in_vmem, in_vmem, pl.BlockSpec(memory_space=pltpu.SMEM), anywhere],
        out_specs=[anywhere, in_vmem, in_vmem],
        scratch_shapes=[
            pltpu.VMEM((TOKENS, FEATURES), BF16),
            pltpu.VMEM((TOKENS, 2 * columns), BF16),
            pltpu.VMEM((TOKENS, columns), BF16),
            pltpu.VMEM((TOKENS, columns), BF16),
            pltpu.VMEM((2 * RANK, FEATURES), BF16),
            pltpu.VMEM((2 * RANK, 2 * columns), BF16),
            pltpu.VMEM((2 * RANK, columns), BF16),
            pltpu.VMEM((TOKENS, 2 * columns), BF16),
            head_store,
            head_store,
            pltpu.VMEM((TOKENS, 2 * columns), BF16),
            pltpu.VMEM((TOKENS // ROWS, ROWS, SPAN), F32),
            pltpu.VMEM((TOKENS, HEAD_SIZE), F32),
            pltpu.VMEM((TOKENS, HEAD_SIZE), F32),
            low_shape,
            low_shape,
            pltpu.VMEM((2 * RANK, TOKENS), BF16),
            pltpu.VMEM((TOKENS, 2 * RANK), BF16),
            low_shape,
            low_shape,
            pltpu.VMEM((TOKENS, PAIR), BF16),
            pltpu.VMEM((HEAD_SIZE, REACH), F32),
            pltpu.VMEM((KV, HEAD_SIZE, TOKENS), F32),
            value_terms,
            value_terms,
            pltpu.VMEM((RANK, GROUP * query_sum[2]), F32),
            pltpu.VMEM((RANK, GROUP * value_sum[2]), F32),
        ]
        + [pltpu.VMEM(shape, BF16) for _ in range(3) for shape in (query_sum, value_sum)]
        + [
            dma((9,)),
            dma((KV,)),
            dma((2,)),
            dma((2, 2)),
        ]
        + [dma((2, KV))] * 6
        + [dma((2, 3, GROUP - 1))] * 2,
        compiler_params=pltpu.CompilerParams(
            collective_id=1, has_side_effects=True, vmem_limit_bytes=56 * 2**20
        ),
    )(
        hidden_states,
        query_base,
        key_base,
        frozen_value_rows,
        query_down.T,
        query_up,
        value_down.T,
        value_up_weight,
        positions.reshape(1, TOKENS),
        turns_of_angles(),
        block_mask.T,
        output_gradient,
    )
    outs = pl.pallas_call(
        output_kernel,
        out_shape=[
            jax.ShapeDtypeStruct((TOKENS, 2 * columns), BF16),
            jax.ShapeDtypeStruct((RANK, FEATURES), F32),
            jax.ShapeDtypeStruct((RANK, 2 * columns), F32),
            jax.ShapeDtypeStruct((RANK, FEATURES), F32),
            jax.ShapeDtypeStruct((RANK, columns), F32),
        ],
        in_specs=[anywhere, in_vmem, in_vmem],
        out_specs=[anywhere] + [in_vmem] * 4,
        scratch_shapes=[pltpu.VMEM((TOKENS, 2 * columns), BF16), dma((2, PIECES))],
        compiler_params=pltpu.CompilerParams(vmem_limit_bytes=56 * 2**20),
    )(passed, final_query, final_value)
    attention_out, down_query, up_query, down_value, up_value = outs
    return attention_out, down_query.T, up_query, down_value.T, up_value


def solution(mesh):
    placed = (
        P("ctx", "head"),
        P("ctx", "head"),
        P("ctx", "head"),
        P("ctx", "head"),
        P("head", None),
        P(None, "head"),
        P("head", None),
        P(None, "head"),
        P("ctx"),
        P(),
        P("ctx", "head"),
    )
    return jax.shard_map(
        per_device,
        mesh=mesh,
        in_specs=placed,
        out_specs=(
            P("ctx", "head"),
            P("head", None),
            P(None, "head"),
            P("head", None),
            P(None, "head"),
        ),
        check_vma=False,
    )
```

```python
import functools
import math

import jax
import jax.numpy as jnp
import numpy as np
from jax import lax
from jax.experimental import pallas as pl
from jax.experimental.pallas import tpu as pltpu
from jax.sharding import PartitionSpec as P

D = 5376
QUERY_HEADS = 32
KEY_VALUE_HEADS = 16
HEAD_SIZE = 128
WINDOW = 1024
BLOCK = 128
ROPE_BASE = 10000.0

TOKENS = 512
FEATURES = 2688
KV = 8
PAIR = 2 * HEAD_SIZE
ROWS = 256
SPAN = WINDOW + ROWS
REACH = WINDOW + TOKENS
AHEAD = 2
LAG = 3
HIDDEN = -1e30
SCALE = (D // QUERY_HEADS) ** -0.5
BF16 = jnp.bfloat16
F32 = jnp.float32

RANK = 16
GROUP = 8
PIECES = 4
MESH = pl.DeviceIdType.MESH


def pieces_of(widths, chunk_width):
    pieces, start = [], 0
    for which, width in enumerate(widths):
        done = 0
        while done < width:
            chunk, inside = divmod(start + done, chunk_width)
            size = min(width - done, chunk_width - inside)
            pieces.append((which, done, chunk, inside, size))
            done += size
        start += width
    return pieces


def turns_of_angles():
    half = HEAD_SIZE // 2
    turns = ROPE_BASE ** (-2.0 * np.arange(half) / HEAD_SIZE) / (2.0 * math.pi)
    mantissa, exponent = np.frexp(turns)
    coarse = np.ldexp(np.floor(mantissa * 256.0), exponent - 8)
    rows = np.stack([np.tile(coarse, 2), np.tile(turns - coarse, 2)])
    return np.concatenate([rows, np.zeros((6, HEAD_SIZE))]).astype(np.float32)


def nearest(x):
    return jnp.floor(x + 0.5)


def sine_of_turns(r):
    r = r - nearest(r)
    r = jnp.where(r > 0.25, 0.5 - r, jnp.where(r < -0.25, -0.5 - r, r))
    x = r * (2.0 * math.pi)
    y = x * x
    out = jnp.full_like(y, -1.0 / math.factorial(11))
    for power in (9, 7, 5, 3, 1):
        sign = 1.0 if power % 4 == 1 else -1.0
        out = out * y + sign / math.factorial(power)
    return out * x


def dot(a, b, contract):
    return lax.dot_general(a, b, ((contract[:1], contract[1:]), ((), ())), preferred_element_type=F32)


def layer_kernel(
    hidden_hbm,
    query_hbm,
    key_hbm,
    value_hbm,
    query_down_hbm,
    query_up_hbm,
    value_down_hbm,
    value_up_hbm,
    positions_ref,
    turns_ref,
    mask_ref,
    gradient_hbm,
    out_hbm,
    final_query,
    final_value,
    hidden,
    query_base,
    key_base,
    value_base,
    downs,
    query_up,
    value_up,
    gradient,
    keys,
    values,
    out,
    bias,
    cosines,
    sines,
    low_mine,
    low_theirs,
    low_rows,
    low_cols,
    back_mine,
    back_theirs,
    query_grad,
    held_weights,
    held_inverse,
    value_sum,
    value_own,
    value_sent,
    value_got,
    row_query,
    row_value,
    parts_query,
    parts_value,
    near_query,
    near_value,
    away_query,
    away_value,
    load_sem,
    out_sem,
    low_sem,
    back_sem,
    far_send,
    far_recv,
    near_send,
    near_recv,
    grad_send,
    grad_recv,
    sum_send,
    sum_recv,
):
    ctx, head = lax.axis_index("ctx"), lax.axis_index("head")
    count = lax.axis_size("ctx")
    core = ctx % 2
    ahead_1, ahead_2 = (ctx + 1) % count, (ctx + 2) % count
    behind_1, behind_2 = (ctx + count - 1) % count, (ctx + count - 2) % count

    def remote(source, target, send, recv, at_ctx, at_head=head):
        return pltpu.make_async_remote_copy(
            src_ref=source,
            dst_ref=target,
            send_sem=send,
            recv_sem=recv,
            device_id=(at_ctx, at_head),
            device_id_type=MESH,
        )

    loads = [
        pltpu.make_async_copy(source, target, load_sem.at[k])
        for k, (source, target) in enumerate(
            (
                (key_hbm, key_base),
                (query_down_hbm, downs.at[0:RANK]),
                (value_down_hbm, downs.at[RANK : 2 * RANK]),
                (hidden_hbm, hidden),
                (value_up_hbm, value_up.at[RANK : 2 * RANK]),
                (value_hbm, value_base),
                (query_up_hbm, query_up.at[0:RANK]),
                (query_hbm, query_base),
                (gradient_hbm, gradient),
            )
        )
    ]
    for one in loads:
        one.start()

    barrier = pltpu.get_barrier_semaphore()
    member, group = ctx % GROUP, ctx // GROUP
    groups = count // GROUP
    near_peers = [group * GROUP + (member + by) % GROUP for by in range(1, GROUP)]
    far_peers = [((group + by) % groups) * GROUP + member for by in range(1, groups)]
    greeted = [(at, head) for at in (ahead_1, ahead_2, behind_1, behind_2)]
    greeted += [(ctx, 1 - head)] + [(at, head) for at in near_peers + far_peers]
    for at in greeted:
        pl.semaphore_signal(barrier, inc=1, device_id=at, device_id_type=MESH)

    lane = lax.broadcasted_iota(jnp.int32, (TOKENS, HEAD_SIZE), 1)
    first_half = lane < HEAD_SIZE // 2
    position = jnp.transpose(
        jnp.broadcast_to(positions_ref[...].astype(F32), (HEAD_SIZE, TOKENS))
    )
    coarse = position * turns_ref[0:1, :]
    fine = position * turns_ref[1:2, :]
    turns = (coarse - nearest(coarse)) + (fine - nearest(fine))
    table = sine_of_turns(turns + jnp.where(first_half, 0.25, 0.0))
    swapped = pltpu.roll(table, HEAD_SIZE // 2, 1)
    cosines[...] = jnp.where(first_half, table, swapped)
    sines[...] = jnp.where(first_half, -swapped, table)

    def rope(x, cos, sin):
        return x * cos + pltpu.roll(x, HEAD_SIZE // 2, 1) * sin

    def turn_keys(h):
        columns = slice(h * HEAD_SIZE, (h + 1) * HEAD_SIZE)
        keys[h, WINDOW:REACH] = rope(
            key_base[:, columns].astype(F32), cosines[...], sines[...]
        ).astype(BF16)

    loads[0].wait()
    for h in range(AHEAD):
        turn_keys(h)

    pl.semaphore_wait(barrier, len(greeted))

    def far_copy(store, kind, h):
        return remote(
            store.at[h, WINDOW:REACH],
            store.at[h, 0:TOKENS],
            far_send.at[kind, h],
            far_recv.at[kind, h],
            ahead_2,
        )

    def near_copy(store, kind, h, first, at_ctx):
        return remote(
            store.at[h, pl.ds(first, TOKENS)],
            store.at[h, TOKENS:WINDOW],
            near_send.at[kind, h],
            near_recv.at[kind, h],
            at_ctx,
        )

    def send_own(store, kind, h):
        @pl.when(ctx + 2 < count)
        def _():
            far_copy(store, kind, h).start()

        @pl.when(core == 0)
        def _():
            near_copy(store, kind, h, WINDOW, ahead_1).start()

    for h in range(AHEAD):
        send_own(keys, 0, h)

    for one in loads[1:4]:
        one.wait()
    low_mine[...] = dot(downs[...], hidden[...], (1, 1))
    low_copy = remote(low_mine, low_theirs, low_sem.at[0], low_sem.at[1], ctx, 1 - head)
    low_copy.start()

    for h in range(AHEAD, KV):
        turn_keys(h)

    key_at = lax.broadcasted_iota(jnp.int32, (BLOCK, BLOCK), 1)
    query_at = lax.broadcasted_iota(jnp.int32, (BLOCK, BLOCK), 0)
    for half in range(TOKENS // ROWS):
        for r in range(ROWS // BLOCK):
            block = ctx * (TOKENS // BLOCK) + half * (ROWS // BLOCK) + r
            for j in range(SPAN // BLOCK):
                offset = WINDOW // BLOCK + r - j
                if 0 <= offset <= WINDOW // BLOCK:
                    seen = (mask_ref[offset, block] == 1) & (block >= offset)
                    tile = jnp.full((BLOCK, BLOCK), jnp.where(seen, 0.0, HIDDEN))
                    if offset == 0:
                        tile = jnp.where(key_at <= query_at, tile, HIDDEN)
                    if offset == WINDOW // BLOCK:
                        tile = jnp.where(key_at > query_at, tile, HIDDEN)
                else:
                    tile = jnp.full((BLOCK, BLOCK), HIDDEN, F32)
                bias[
                    half, r * BLOCK : (r + 1) * BLOCK, j * BLOCK : (j + 1) * BLOCK
                ] = tile

    query_up[RANK : 2 * RANK] = jnp.zeros((RANK, KV * PAIR), BF16)
    value_up[0:RANK] = jnp.zeros((RANK, KV * HEAD_SIZE), BF16)
    back_mine[...] = jnp.zeros_like(back_mine)
    for padded, used in ((row_query, FEATURES + KV * PAIR), (row_value, FEATURES + KV * HEAD_SIZE)):
        padded[:, used:] = jnp.zeros((RANK, padded.shape[1] - used), F32)

    @pl.when(ctx < 2)
    def _():
        for store in (keys, values):
            store[:, 0:TOKENS] = jnp.zeros((KV, TOKENS, HEAD_SIZE), BF16)

    @pl.when(ctx < 1)
    def _():
        for store in (keys, values):
            store[:, TOKENS:WINDOW] = jnp.zeros((KV, TOKENS, HEAD_SIZE), BF16)

    @pl.when(ctx + 2 >= count)
    def _():
        value_got[:, 1] = jnp.zeros((KV, HEAD_SIZE, TOKENS), BF16)

    @pl.when(ctx + 1 >= count)
    def _():
        value_got[:, 0] = jnp.zeros((KV, HEAD_SIZE, TOKENS), BF16)

    low_copy.wait_recv()
    low = low_mine[...] + low_theirs[...]
    low_rows[...] = low.astype(BF16)
    low_cols[...] = jnp.transpose(low).astype(BF16)
    loads[4].wait()
    loads[5].wait()
    for h in range(KV):
        columns = slice(h * HEAD_SIZE, (h + 1) * HEAD_SIZE)
        values[h, WINDOW:REACH] = (
            value_base[:, columns].astype(F32) + dot(low_cols[...], value_up[:, columns], (1, 0))
        ).astype(BF16)
        if h < AHEAD - 1:
            send_own(values, 1, h)
    for one in loads[6:]:
        one.wait()

    def out_copy(h):
        columns = pl.ds(pl.multiple_of(h * PAIR, PAIR), PAIR)
        return pltpu.make_async_copy(out.at[:, columns], out_hbm.at[:, columns], out_sem.at[h])

    def grad_copy(kind, h):
        return remote(
            value_sent.at[h, kind],
            value_got.at[h, kind],
            grad_send.at[kind, h],
            grad_recv.at[kind, h],
            behind_1 if kind == 0 else behind_2,
        )

    def stack(x):
        return jnp.concatenate([x[:, :HEAD_SIZE], x[:, HEAD_SIZE:]], axis=0)

    def beside(x):
        return jnp.concatenate([x[:ROWS], x[ROWS:]], axis=1)

    def send_terms(h):
        value_sent[h, 1] = value_sum[:, 0:TOKENS].astype(BF16)
        value_sent[h, 0] = value_sum[:, TOKENS:WINDOW].astype(BF16)

        @pl.when(ctx >= 2)
        def _():
            grad_copy(1, h).start()

        @pl.when(ctx >= 1)
        def _():
            grad_copy(0, h).start()

        value_own[h] = value_sum[:, WINDOW:REACH]

    halves = range(TOKENS // ROWS)
    rows = [slice(half * ROWS, (half + 1) * ROWS) for half in halves]
    span = [slice(half * ROWS, half * ROWS + SPAN) for half in halves]

    def twice(x):
        return jnp.concatenate([x, x], axis=0)

    def pair_of(h):
        return pl.ds(pl.multiple_of(h * PAIR, PAIR), PAIR)

    def key_part(h):
        pair = pair_of(h)

        def score(half):
            raw = query_base[rows[half], pair].astype(F32) + dot(
                low_cols[rows[half]], query_up[:, pair], (1, 0)
            )
            queries = rope(stack(raw), twice(cosines[rows[half]]), twice(sines[rows[half]]))
            queries = queries * (SCALE * math.log2(math.e))
            return dot(queries.astype(BF16), keys[h, span[half]], (1, 1))

        def weigh(half, scores):
            scores = (
                scores.reshape(2, ROWS, SPAN) + bias[half][None]
            ).reshape(2 * ROWS, SPAN)
            weights = jnp.exp2(scores - jnp.max(scores, axis=1, keepdims=True))
            inverse = 1.0 / jnp.sum(weights, axis=1, keepdims=True)
            weights = weights.astype(BF16)
            held_weights[h % 2, half] = weights
            held_inverse[h % 2, half] = jnp.broadcast_to(inverse, (2 * ROWS, HEAD_SIZE))
            out_grad = stack(gradient[rows[half], pair]).astype(F32)
            terms = dot((out_grad * inverse).astype(BF16), weights, (0, 0))
            if half == 0:
                value_sum[:, 0:SPAN] = terms
            else:
                value_sum[:, ROWS:SPAN] += terms[:, : SPAN - ROWS]
                value_sum[:, SPAN:REACH] = terms[:, SPAN - ROWS :]

        scores = [score(half) for half in halves]
        for half in halves:
            weigh(half, scores[half])
        send_terms(h)

    def value_part(h):
        pair = pair_of(h)

        def attend(half):
            result = dot(held_weights[h % 2, half], values[h, span[half]], (1, 0))
            result = (result * held_inverse[h % 2, half]).astype(BF16)
            out[rows[half], pair] = beside(result)
            return result

        def grad(half):
            return dot(stack(gradient[rows[half], pair]), values[h, span[half]], (1, 1))

        def back(half, grad_weights, result):
            out_grad = stack(gradient[rows[half], pair]).astype(F32)
            delta = jnp.sum(out_grad * result.astype(F32), axis=1, keepdims=True)
            grad_scores = held_weights[h % 2, half] * (grad_weights - delta).astype(BF16)
            turned = rope(
                dot(grad_scores, keys[h, span[half]], (1, 0))
                * (held_inverse[h % 2, half] * SCALE),
                twice(cosines[rows[half]]),
                -twice(sines[rows[half]]),
            )
            query_grad[rows[half]] = beside(turned.astype(BF16))

        results = [attend(half) for half in halves]
        grads = [grad(half) for half in halves]
        for half in halves:
            back(half, grads[half], results[half])
        out_copy(h).start()
        back_mine[0:RANK] += dot(query_up[0:RANK, pair], query_grad[...], (1, 1))
        row_query[:, pl.ds(pl.multiple_of(h * PAIR, HEAD_SIZE) + FEATURES, PAIR)] = dot(
            low_rows[0:RANK], query_grad[...], (1, 0)
        )

    def pass_on(store, kind, h):
        @pl.when(ctx >= 2)
        def _():
            far_copy(store, kind, h).wait_recv()

        @pl.when((core == 1) & (ctx >= 2))
        def _():
            near_copy(store, kind, h, 0, behind_1).start()

    def arrived(store, kind, h):
        @pl.when(ctx >= 1)
        def _():
            near_copy(store, kind, h, 0, behind_1).wait_recv()

    def absorb(h):
        @pl.when(ctx + 1 < count)
        def _():
            grad_copy(0, h).wait_recv()

        @pl.when(ctx + 2 < count)
        def _():
            grad_copy(1, h).wait_recv()

        total = (
            value_own[h] + value_got[h, 0].astype(F32) + value_got[h, 1].astype(F32)
        ).astype(BF16)
        columns = pl.ds(pl.multiple_of(h * HEAD_SIZE, HEAD_SIZE), HEAD_SIZE)
        back_mine[RANK : 2 * RANK] += dot(value_up[RANK : 2 * RANK, columns], total, (1, 0))
        row_value[:, pl.ds(pl.multiple_of(h * HEAD_SIZE, HEAD_SIZE) + FEATURES, HEAD_SIZE)] = dot(
            low_rows[RANK : 2 * RANK], total, (1, 1)
        )

    def one_head(h, carry):
        @pl.when(h + AHEAD < KV)
        def _():
            send_own(keys, 0, h + AHEAD)

        @pl.when(h + AHEAD - 1 < KV)
        def _():
            send_own(values, 1, h + AHEAD - 1)

        pass_on(keys, 0, h)
        arrived(keys, 0, h)
        key_part(h)

        @pl.when(h >= 1)
        def _():
            pass_on(values, 1, h - 1)
            arrived(values, 1, h - 1)
            value_part(h - 1)

        @pl.when(h >= LAG)
        def _():
            absorb(h - LAG)

        return carry

    lax.fori_loop(0, KV, one_head, 0)
    pass_on(values, 1, KV - 1)

    def back_copy(kind):
        rows = pl.ds(kind * RANK, RANK)
        return remote(
            back_mine.at[rows],
            back_theirs.at[rows],
            back_sem.at[0, kind],
            back_sem.at[1, kind],
            ctx,
            1 - head,
        )

    stores = (
        (row_query, parts_query, near_query, away_query, final_query),
        (row_value, parts_value, near_value, away_value, final_value),
    )

    def sum_copy(kind, step, k, peer):
        _, parts, near, away, final = stores[kind]
        source, target = (
            (parts.at[peer % GROUP], near.at[k]),
            (away.at[group], away.at[group]),
            (final.at[member], final.at[member]),
        )[step]
        return remote(
            source, target, sum_send.at[kind, step, k], sum_recv.at[kind, step, k], peer
        )

    def sum_copies(kind, step):
        peers = far_peers if step == 1 else near_peers
        return [sum_copy(kind, step, k, peer) for k, peer in enumerate(peers)]

    def scatter(kind):
        row, parts = stores[kind][:2]
        rows = slice(kind * RANK, (kind + 1) * RANK)
        back_copy(kind).wait_recv()
        total = (back_mine[rows] + back_theirs[rows]).astype(BF16)
        row[:, 0:FEATURES] = dot(total, hidden[...], (1, 0))
        width = parts.shape[2]
        for k in range(GROUP):
            parts[k] = row[:, k * width : (k + 1) * width].astype(BF16)
        for one in sum_copies(kind, 0):
            one.start()

    def exchange(kind):
        _, parts, near, away, _ = stores[kind]
        total = parts[member].astype(F32)
        for k, one in enumerate(sum_copies(kind, 0)):
            one.wait_recv()
            total += near[k].astype(F32)
        away[group] = total.astype(BF16)
        for one in sum_copies(kind, 1):
            one.start()

    def gather(kind):
        away, final = stores[kind][3:]
        for one in sum_copies(kind, 1):
            one.wait_recv()
        total = away[0].astype(F32)
        for k in range(1, groups):
            total += away[k].astype(F32)
        final[member] = (total * (TOKENS * count) ** -0.5).astype(BF16)
        for one in sum_copies(kind, 2):
            one.start()

    for h in range(KV - LAG, KV - 1):
        absorb(h)
    arrived(values, 1, KV - 1)
    value_part(KV - 1)
    back_copy(0).start()
    absorb(KV - 1)
    back_copy(1).start()
    scatter(0)
    scatter(1)
    exchange(0)
    exchange(1)
    gather(0)
    gather(1)
    low_copy.wait_send()
    for kind in range(2):
        for one in sum_copies(kind, 2):
            one.wait_recv()
        for step in range(3):
            for one in sum_copies(kind, step):
                one.wait_send()
        back_copy(kind).wait_send()

    def finish(h, carry):
        @pl.when(ctx + 2 < count)
        def _():
            far_copy(keys, 0, h).wait_send()
            far_copy(values, 1, h).wait_send()

        @pl.when((core == 0) | (ctx >= 2))
        def _():
            near_copy(keys, 0, h, 0, behind_1).wait_send()
            near_copy(values, 1, h, 0, behind_1).wait_send()

        @pl.when(ctx >= 1)
        def _():
            grad_copy(0, h).wait_send()

        @pl.when(ctx >= 2)
        def _():
            grad_copy(1, h).wait_send()

        out_copy(h).wait()
        return carry

    lax.fori_loop(0, KV, finish, 0)


def output_kernel(
    passed,
    final_query,
    final_value,
    attention_out,
    down_query,
    up_query,
    down_value,
    up_value,
    held,
    sem,
):
    size = TOKENS // PIECES

    def copy(k, step):
        piece = pl.ds(k * size, size)
        source, target = ((passed, held), (held, attention_out))[step]
        return pltpu.make_async_copy(source.at[piece], target.at[piece], sem.at[step, k])

    for k in range(PIECES):
        copy(k, 0).start()
    for k in range(PIECES):
        copy(k, 0).wait()
        copy(k, 1).start()
    for final, outs in ((final_query, (down_query, up_query)), (final_value, (down_value, up_value))):
        width = final.shape[2]
        for which, at, chunk, inside, size in pieces_of([o.shape[1] for o in outs], width):
            outs[which][:, at : at + size] = final[chunk, :, inside : inside + size].astype(F32)
    for k in range(PIECES):
        copy(k, 1).wait()


def per_device(
    hidden_states,
    query_base,
    key_base,
    frozen_value_rows,
    query_down,
    query_up,
    value_down,
    value_up_weight,
    positions,
    block_mask,
    output_gradient,
):
    anywhere = pl.BlockSpec(memory_space=pl.ANY)
    in_vmem = pl.BlockSpec(memory_space=pltpu.VMEM)
    columns = KV * HEAD_SIZE
    head_store = pltpu.VMEM((KV, REACH, HEAD_SIZE), BF16)
    value_terms = pltpu.VMEM((KV, 2, HEAD_SIZE, TOKENS), BF16)
    low_shape = pltpu.VMEM((2 * RANK, TOKENS), F32)
    query_sum = (GROUP, RANK, 5 * HEAD_SIZE)
    value_sum = (GROUP, RANK, 4 * HEAD_SIZE)
    dma = pltpu.SemaphoreType.DMA
    passed, final_query, final_value = pl.pallas_call(
        layer_kernel,
        out_shape=[
            jax.ShapeDtypeStruct((TOKENS, 2 * columns), BF16),
            jax.ShapeDtypeStruct(query_sum, BF16),
            jax.ShapeDtypeStruct(value_sum, BF16),
        ],
        in_specs=[anywhere] * 8
        + [in_vmem, in_vmem, pl.BlockSpec(memory_space=pltpu.SMEM), anywhere],
        out_specs=[anywhere, in_vmem, in_vmem],
        scratch_shapes=[
            pltpu.VMEM((TOKENS, FEATURES), BF16),
            pltpu.VMEM((TOKENS, 2 * columns), BF16),
            pltpu.VMEM((TOKENS, columns), BF16),
            pltpu.VMEM((TOKENS, columns), BF16),
            pltpu.VMEM((2 * RANK, FEATURES), BF16),
            pltpu.VMEM((2 * RANK, 2 * columns), BF16),
            pltpu.VMEM((2 * RANK, columns), BF16),
            pltpu.VMEM((TOKENS, 2 * columns), BF16),
            head_store,
            head_store,
            pltpu.VMEM((TOKENS, 2 * columns), BF16),
            pltpu.VMEM((TOKENS // ROWS, ROWS, SPAN), F32),
            pltpu.VMEM((TOKENS, HEAD_SIZE), F32),
            pltpu.VMEM((TOKENS, HEAD_SIZE), F32),
            low_shape,
            low_shape,
            pltpu.VMEM((2 * RANK, TOKENS), BF16),
            pltpu.VMEM((TOKENS, 2 * RANK), BF16),
            low_shape,
            low_shape,
            pltpu.VMEM((TOKENS, PAIR), BF16),
            pltpu.VMEM((2, TOKENS // ROWS, 2 * ROWS, SPAN), BF16),
            pltpu.VMEM((2, TOKENS // ROWS, 2 * ROWS, HEAD_SIZE), F32),
            pltpu.VMEM((HEAD_SIZE, REACH), F32),
            pltpu.VMEM((KV, HEAD_SIZE, TOKENS), F32),
            value_terms,
            value_terms,
            pltpu.VMEM((RANK, GROUP * query_sum[2]), F32),
            pltpu.VMEM((RANK, GROUP * value_sum[2]), F32),
        ]
        + [pltpu.VMEM(shape, BF16) for _ in range(3) for shape in (query_sum, value_sum)]
        + [
            dma((9,)),
            dma((KV,)),
            dma((2,)),
            dma((2, 2)),
        ]
        + [dma((2, KV))] * 6
        + [dma((2, 3, GROUP - 1))] * 2,
        compiler_params=pltpu.CompilerParams(
            collective_id=1, has_side_effects=True, vmem_limit_bytes=56 * 2**20
        ),
    )(
        hidden_states,
        query_base,
        key_base,
        frozen_value_rows,
        query_down.T,
        query_up,
        value_down.T,
        value_up_weight,
        positions.reshape(1, TOKENS),
        turns_of_angles(),
        block_mask.T,
        output_gradient,
    )
    outs = pl.pallas_call(
        output_kernel,
        out_shape=[
            jax.ShapeDtypeStruct((TOKENS, 2 * columns), BF16),
            jax.ShapeDtypeStruct((RANK, FEATURES), F32),
            jax.ShapeDtypeStruct((RANK, 2 * columns), F32),
            jax.ShapeDtypeStruct((RANK, FEATURES), F32),
            jax.ShapeDtypeStruct((RANK, columns), F32),
        ],
        in_specs=[anywhere, in_vmem, in_vmem],
        out_specs=[anywhere] + [in_vmem] * 4,
        scratch_shapes=[pltpu.VMEM((TOKENS, 2 * columns), BF16), dma((2, PIECES))],
        compiler_params=pltpu.CompilerParams(vmem_limit_bytes=56 * 2**20),
    )(passed, final_query, final_value)
    attention_out, down_query, up_query, down_value, up_value = outs
    return attention_out, down_query.T, up_query, down_value.T, up_value


def solution(mesh):
    placed = (
        P("ctx", "head"),
        P("ctx", "head"),
        P("ctx", "head"),
        P("ctx", "head"),
        P("head", None),
        P(None, "head"),
        P("head", None),
        P(None, "head"),
        P("ctx"),
        P(),
        P("ctx", "head"),
    )
    return jax.shard_map(
        per_device,
        mesh=mesh,
        in_specs=placed,
        out_specs=(
            P("ctx", "head"),
            P("head", None),
            P(None, "head"),
            P("head", None),
            P(None, "head"),
        ),
        check_vma=False,
    )
```

```python
import functools
import math

import jax
import jax.numpy as jnp
import numpy as np
from jax import lax
from jax.experimental import pallas as pl
from jax.experimental.pallas import tpu as pltpu
from jax.sharding import PartitionSpec as P

D = 5376
QUERY_HEADS = 32
KEY_VALUE_HEADS = 16
HEAD_SIZE = 128
WINDOW = 1024
BLOCK = 128
ROPE_BASE = 10000.0

TOKENS = 512
FEATURES = 2688
KV = 8
PAIR = 2 * HEAD_SIZE
ROWS = 256
SPAN = WINDOW + ROWS
REACH = WINDOW + TOKENS
AHEAD = 2
LAG = 3
HIDDEN = -1e30
SCALE = (D // QUERY_HEADS) ** -0.5
BF16 = jnp.bfloat16
F32 = jnp.float32

RANK = 16
GROUP = 8
PIECES = 4
MESH = pl.DeviceIdType.MESH


def pieces_of(widths, chunk_width):
    pieces, start = [], 0
    for which, width in enumerate(widths):
        done = 0
        while done < width:
            chunk, inside = divmod(start + done, chunk_width)
            size = min(width - done, chunk_width - inside)
            pieces.append((which, done, chunk, inside, size))
            done += size
        start += width
    return pieces


def turns_of_angles():
    half = HEAD_SIZE // 2
    turns = ROPE_BASE ** (-2.0 * np.arange(half) / HEAD_SIZE) / (2.0 * math.pi)
    mantissa, exponent = np.frexp(turns)
    coarse = np.ldexp(np.floor(mantissa * 256.0), exponent - 8)
    rows = np.stack([np.tile(coarse, 2), np.tile(turns - coarse, 2)])
    return np.concatenate([rows, np.zeros((6, HEAD_SIZE))]).astype(np.float32)


def nearest(x):
    return jnp.floor(x + 0.5)


def sine_of_turns(r):
    r = r - nearest(r)
    r = jnp.where(r > 0.25, 0.5 - r, jnp.where(r < -0.25, -0.5 - r, r))
    x = r * (2.0 * math.pi)
    y = x * x
    out = jnp.full_like(y, -1.0 / math.factorial(11))
    for power in (9, 7, 5, 3, 1):
        sign = 1.0 if power % 4 == 1 else -1.0
        out = out * y + sign / math.factorial(power)
    return out * x


def dot(a, b, contract):
    return lax.dot_general(a, b, ((contract[:1], contract[1:]), ((), ())), preferred_element_type=F32)


def layer_kernel(
    hidden_hbm,
    query_hbm,
    key_hbm,
    value_hbm,
    query_down_hbm,
    query_up_hbm,
    value_down_hbm,
    value_up_hbm,
    positions_ref,
    turns_ref,
    mask_ref,
    gradient_hbm,
    out_hbm,
    final_query,
    final_value,
    hidden,
    query_base,
    key_base,
    value_base,
    downs,
    query_up,
    value_up,
    gradient,
    keys,
    values,
    out,
    bias,
    cosines,
    sines,
    low_mine,
    low_theirs,
    low_rows,
    low_cols,
    back_mine,
    back_theirs,
    query_grad,
    held_weights,
    held_inverse,
    value_sum,
    value_own,
    value_sent,
    value_got,
    row_query,
    row_value,
    parts_query,
    parts_value,
    near_query,
    near_value,
    away_query,
    away_value,
    load_sem,
    out_sem,
    low_sem,
    back_sem,
    far_send,
    far_recv,
    near_send,
    near_recv,
    grad_send,
    grad_recv,
    sum_send,
    sum_recv,
):
    ctx, head = lax.axis_index("ctx"), lax.axis_index("head")
    count = lax.axis_size("ctx")
    core = ctx % 2
    ahead_1, ahead_2 = (ctx + 1) % count, (ctx + 2) % count
    behind_1, behind_2 = (ctx + count - 1) % count, (ctx + count - 2) % count

    def remote(source, target, send, recv, at_ctx, at_head=head):
        return pltpu.make_async_remote_copy(
            src_ref=source,
            dst_ref=target,
            send_sem=send,
            recv_sem=recv,
            device_id=(at_ctx, at_head),
            device_id_type=MESH,
        )

    loads = [
        pltpu.make_async_copy(source, target, load_sem.at[k])
        for k, (source, target) in enumerate(
            (
                (key_hbm, key_base),
                (query_down_hbm, downs.at[0:RANK]),
                (value_down_hbm, downs.at[RANK : 2 * RANK]),
                (hidden_hbm, hidden),
                (value_up_hbm, value_up.at[RANK : 2 * RANK]),
                (value_hbm, value_base),
                (query_up_hbm, query_up.at[0:RANK]),
                (query_hbm, query_base),
                (gradient_hbm, gradient),
            )
        )
    ]
    for one in loads:
        one.start()

    barrier = pltpu.get_barrier_semaphore()
    member, group = ctx % GROUP, ctx // GROUP
    groups = count // GROUP
    near_peers = [group * GROUP + (member + by) % GROUP for by in range(1, GROUP)]
    far_peers = [((group + by) % groups) * GROUP + member for by in range(1, groups)]
    greeted = [(at, head) for at in (ahead_1, ahead_2, behind_1, behind_2)]
    greeted += [(ctx, 1 - head)] + [(at, head) for at in near_peers + far_peers]
    for at in greeted:
        pl.semaphore_signal(barrier, inc=1, device_id=at, device_id_type=MESH)

    lane = lax.broadcasted_iota(jnp.int32, (TOKENS, HEAD_SIZE), 1)
    first_half = lane < HEAD_SIZE // 2
    position = jnp.transpose(
        jnp.broadcast_to(positions_ref[...].astype(F32), (HEAD_SIZE, TOKENS))
    )
    coarse = position * turns_ref[0:1, :]
    fine = position * turns_ref[1:2, :]
    turns = (coarse - nearest(coarse)) + (fine - nearest(fine))
    table = sine_of_turns(turns + jnp.where(first_half, 0.25, 0.0))
    swapped = pltpu.roll(table, HEAD_SIZE // 2, 1)
    cosines[...] = jnp.where(first_half, table, swapped)
    sines[...] = jnp.where(first_half, -swapped, table)

    def rope(x, cos, sin):
        return x * cos + pltpu.roll(x, HEAD_SIZE // 2, 1) * sin

    def turn_keys(h):
        columns = slice(h * HEAD_SIZE, (h + 1) * HEAD_SIZE)
        keys[h, WINDOW:REACH] = rope(
            key_base[:, columns].astype(F32), cosines[...], sines[...]
        ).astype(BF16)

    loads[0].wait()
    for h in range(AHEAD):
        turn_keys(h)

    pl.semaphore_wait(barrier, len(greeted))

    def far_copy(store, kind, h):
        return remote(
            store.at[h, WINDOW:REACH],
            store.at[h, 0:TOKENS],
            far_send.at[kind, h],
            far_recv.at[kind, h],
            ahead_2,
        )

    def near_copy(store, kind, h, first, at_ctx):
        return remote(
            store.at[h, pl.ds(first, TOKENS)],
            store.at[h, TOKENS:WINDOW],
            near_send.at[kind, h],
            near_recv.at[kind, h],
            at_ctx,
        )

    def send_own(store, kind, h):
        @pl.when(ctx + 2 < count)
        def _():
            far_copy(store, kind, h).start()

        @pl.when(core == 0)
        def _():
            near_copy(store, kind, h, WINDOW, ahead_1).start()

    for h in range(AHEAD):
        send_own(keys, 0, h)

    for one in loads[1:4]:
        one.wait()
    low_mine[...] = dot(downs[...], hidden[...], (1, 1))
    low_copy = remote(low_mine, low_theirs, low_sem.at[0], low_sem.at[1], ctx, 1 - head)
    low_copy.start()

    for h in range(AHEAD, KV):
        turn_keys(h)

    key_at = lax.broadcasted_iota(jnp.int32, (BLOCK, BLOCK), 1)
    query_at = lax.broadcasted_iota(jnp.int32, (BLOCK, BLOCK), 0)
    for half in range(TOKENS // ROWS):
        for r in range(ROWS // BLOCK):
            block = ctx * (TOKENS // BLOCK) + half * (ROWS // BLOCK) + r
            for j in range(SPAN // BLOCK):
                offset = WINDOW // BLOCK + r - j
                if 0 <= offset <= WINDOW // BLOCK:
                    seen = (mask_ref[offset, block] == 1) & (block >= offset)
                    tile = jnp.full((BLOCK, BLOCK), jnp.where(seen, 0.0, HIDDEN))
                    if offset == 0:
                        tile = jnp.where(key_at <= query_at, tile, HIDDEN)
                    if offset == WINDOW // BLOCK:
                        tile = jnp.where(key_at > query_at, tile, HIDDEN)
                else:
                    tile = jnp.full((BLOCK, BLOCK), HIDDEN, F32)
                bias[
                    half, r * BLOCK : (r + 1) * BLOCK, j * BLOCK : (j + 1) * BLOCK
                ] = tile

    query_up[RANK : 2 * RANK] = jnp.zeros((RANK, KV * PAIR), BF16)
    value_up[0:RANK] = jnp.zeros((RANK, KV * HEAD_SIZE), BF16)
    back_mine[...] = jnp.zeros_like(back_mine)
    for padded, used in ((row_query, FEATURES + KV * PAIR), (row_value, FEATURES + KV * HEAD_SIZE)):
        padded[:, used:] = jnp.zeros((RANK, padded.shape[1] - used), F32)

    @pl.when(ctx < 2)
    def _():
        for store in (keys, values):
            store[:, 0:TOKENS] = jnp.zeros((KV, TOKENS, HEAD_SIZE), BF16)

    @pl.when(ctx < 1)
    def _():
        for store in (keys, values):
            store[:, TOKENS:WINDOW] = jnp.zeros((KV, TOKENS, HEAD_SIZE), BF16)

    @pl.when(ctx + 2 >= count)
    def _():
        value_got[:, 1] = jnp.zeros((KV, HEAD_SIZE, TOKENS), BF16)

    @pl.when(ctx + 1 >= count)
    def _():
        value_got[:, 0] = jnp.zeros((KV, HEAD_SIZE, TOKENS), BF16)

    low_copy.wait_recv()
    low = low_mine[...] + low_theirs[...]
    low_rows[...] = low.astype(BF16)
    low_cols[...] = jnp.transpose(low).astype(BF16)
    loads[4].wait()
    loads[5].wait()
    for h in range(KV):
        columns = slice(h * HEAD_SIZE, (h + 1) * HEAD_SIZE)
        values[h, WINDOW:REACH] = (
            value_base[:, columns].astype(F32) + dot(low_cols[...], value_up[:, columns], (1, 0))
        ).astype(BF16)
        if h < AHEAD - 1:
            send_own(values, 1, h)
    for one in loads[6:]:
        one.wait()

    def out_copy(h):
        columns = pl.ds(pl.multiple_of(h * PAIR, PAIR), PAIR)
        return pltpu.make_async_copy(out.at[:, columns], out_hbm.at[:, columns], out_sem.at[h])

    def grad_copy(kind, h):
        return remote(
            value_sent.at[h, kind],
            value_got.at[h, kind],
            grad_send.at[kind, h],
            grad_recv.at[kind, h],
            behind_1 if kind == 0 else behind_2,
        )

    def stack(x):
        return jnp.concatenate([x[:, :HEAD_SIZE], x[:, HEAD_SIZE:]], axis=0)

    def beside(x):
        return jnp.concatenate([x[:ROWS], x[ROWS:]], axis=1)

    def send_terms(h):
        value_sent[h, 1] = value_sum[:, 0:TOKENS].astype(BF16)
        value_sent[h, 0] = value_sum[:, TOKENS:WINDOW].astype(BF16)

        @pl.when(ctx >= 2)
        def _():
            grad_copy(1, h).start()

        @pl.when(ctx >= 1)
        def _():
            grad_copy(0, h).start()

        value_own[h] = value_sum[:, WINDOW:REACH]

    halves = range(TOKENS // ROWS)
    rows = [slice(half * ROWS, (half + 1) * ROWS) for half in halves]
    span = [slice(half * ROWS, half * ROWS + SPAN) for half in halves]

    def twice(x):
        return jnp.concatenate([x, x], axis=0)

    def pair_of(h):
        return pl.ds(pl.multiple_of(h * PAIR, PAIR), PAIR)

    def key_part(h):
        pair = pair_of(h)

        def score(half):
            raw = query_base[rows[half], pair].astype(F32) + dot(
                low_cols[rows[half]], query_up[:, pair], (1, 0)
            )
            queries = rope(stack(raw), twice(cosines[rows[half]]), twice(sines[rows[half]]))
            queries = queries * (SCALE * math.log2(math.e))
            return dot(queries.astype(BF16), keys[h, span[half]], (1, 1))

        def weigh(half, scores):
            scores = (
                scores.reshape(2, ROWS, SPAN) + bias[half][None]
            ).reshape(2 * ROWS, SPAN)
            weights = jnp.exp2(scores - jnp.max(scores, axis=1, keepdims=True))
            inverse = 1.0 / jnp.sum(weights, axis=1, keepdims=True)
            weights = weights.astype(BF16)
            held_weights[h % 2, half] = weights
            held_inverse[h % 2, half] = jnp.broadcast_to(inverse, (2 * ROWS, HEAD_SIZE))
            out_grad = stack(gradient[rows[half], pair]).astype(F32)
            terms = dot((out_grad * inverse).astype(BF16), weights, (0, 0))
            if half == 0:
                value_sum[:, 0:SPAN] = terms
            else:
                value_sum[:, ROWS:SPAN] += terms[:, : SPAN - ROWS]
                value_sum[:, SPAN:REACH] = terms[:, SPAN - ROWS :]

        scores = [score(half) for half in halves]
        for half in halves:
            weigh(half, scores[half])
        send_terms(h)

    def value_part(h):
        pair = pair_of(h)

        def attend(half):
            result = dot(held_weights[h % 2, half], values[h, span[half]], (1, 0))
            result = (result * held_inverse[h % 2, half]).astype(BF16)
            out[rows[half], pair] = beside(result)
            return result

        def grad(half):
            return dot(stack(gradient[rows[half], pair]), values[h, span[half]], (1, 1))

        def back(half, grad_weights, result):
            out_grad = stack(gradient[rows[half], pair]).astype(F32)
            delta = jnp.sum(out_grad * result.astype(F32), axis=1, keepdims=True)
            grad_scores = held_weights[h % 2, half] * (grad_weights - delta).astype(BF16)
            turned = rope(
                dot(grad_scores, keys[h, span[half]], (1, 0))
                * (held_inverse[h % 2, half] * SCALE),
                twice(cosines[rows[half]]),
                -twice(sines[rows[half]]),
            )
            query_grad[rows[half]] = beside(turned.astype(BF16))

        results = [attend(half) for half in halves]
        grads = [grad(half) for half in halves]
        for half in halves:
            back(half, grads[half], results[half])
        out_copy(h).start()
        back_mine[0:RANK] += dot(query_up[0:RANK, pair], query_grad[...], (1, 1))
        row_query[:, pl.ds(pl.multiple_of(h * PAIR, HEAD_SIZE) + FEATURES, PAIR)] = dot(
            low_rows[0:RANK], query_grad[...], (1, 0)
        )

    def pass_on(store, kind, h):
        @pl.when(ctx >= 2)
        def _():
            far_copy(store, kind, h).wait_recv()

        @pl.when((core == 1) & (ctx >= 2))
        def _():
            near_copy(store, kind, h, 0, behind_1).start()

    def arrived(store, kind, h):
        @pl.when(ctx >= 1)
        def _():
            near_copy(store, kind, h, 0, behind_1).wait_recv()

    def absorb(h):
        @pl.when(ctx + 1 < count)
        def _():
            grad_copy(0, h).wait_recv()

        @pl.when(ctx + 2 < count)
        def _():
            grad_copy(1, h).wait_recv()

        total = (
            value_own[h] + value_got[h, 0].astype(F32) + value_got[h, 1].astype(F32)
        ).astype(BF16)
        columns = pl.ds(pl.multiple_of(h * HEAD_SIZE, HEAD_SIZE), HEAD_SIZE)
        back_mine[RANK : 2 * RANK] += dot(value_up[RANK : 2 * RANK, columns], total, (1, 0))
        row_value[:, pl.ds(pl.multiple_of(h * HEAD_SIZE, HEAD_SIZE) + FEATURES, HEAD_SIZE)] = dot(
            low_rows[RANK : 2 * RANK], total, (1, 1)
        )

    def one_head(h, carry):
        @pl.when(h + AHEAD < KV)
        def _():
            send_own(keys, 0, h + AHEAD)

        @pl.when(h + AHEAD - 1 < KV)
        def _():
            send_own(values, 1, h + AHEAD - 1)

        pass_on(keys, 0, h)
        arrived(keys, 0, h)
        key_part(h)

        @pl.when(h >= 1)
        def _():
            pass_on(values, 1, h - 1)
            arrived(values, 1, h - 1)
            value_part(h - 1)

        @pl.when(h >= LAG)
        def _():
            absorb(h - LAG)

        return carry

    lax.fori_loop(0, KV, one_head, 0)
    pass_on(values, 1, KV - 1)

    def back_copy(kind):
        rows = pl.ds(kind * RANK, RANK)
        return remote(
            back_mine.at[rows],
            back_theirs.at[rows],
            back_sem.at[0, kind],
            back_sem.at[1, kind],
            ctx,
            1 - head,
        )

    stores = (
        (row_query, parts_query, near_query, away_query, final_query),
        (row_value, parts_value, near_value, away_value, final_value),
    )

    def sum_copy(kind, step, k, peer):
        _, parts, near, away, final = stores[kind]
        source, target = (
            (parts.at[peer % GROUP], near.at[k]),
            (away.at[group], away.at[group]),
            (final.at[member], final.at[member]),
        )[step]
        return remote(
            source, target, sum_send.at[kind, step, k], sum_recv.at[kind, step, k], peer
        )

    def sum_copies(kind, step):
        peers = far_peers if step == 1 else near_peers
        return [sum_copy(kind, step, k, peer) for k, peer in enumerate(peers)]

    def scatter(kind):
        row, parts = stores[kind][:2]
        rows = slice(kind * RANK, (kind + 1) * RANK)
        back_copy(kind).wait_recv()
        total = (back_mine[rows] + back_theirs[rows]).astype(BF16)
        row[:, 0:FEATURES] = dot(total, hidden[...], (1, 0))
        width = parts.shape[2]
        for k in range(GROUP):
            parts[k] = row[:, k * width : (k + 1) * width].astype(BF16)
        for one in sum_copies(kind, 0):
            one.start()

    def exchange(kind):
        _, parts, near, away, _ = stores[kind]
        total = parts[member].astype(F32)
        for k, one in enumerate(sum_copies(kind, 0)):
            one.wait_recv()
            total += near[k].astype(F32)
        away[group] = total.astype(BF16)
        for one in sum_copies(kind, 1):
            one.start()

    def gather(kind):
        away, final = stores[kind][3:]
        for one in sum_copies(kind, 1):
            one.wait_recv()
        total = away[0].astype(F32)
        for k in range(1, groups):
            total += away[k].astype(F32)
        final[member] = (total * (TOKENS * count) ** -0.5).astype(BF16)
        for one in sum_copies(kind, 2):
            one.start()

    for h in range(KV - LAG, KV - 1):
        absorb(h)
    arrived(values, 1, KV - 1)
    value_part(KV - 1)
    back_copy(0).start()
    absorb(KV - 1)
    back_copy(1).start()
    scatter(0)
    scatter(1)
    exchange(0)
    exchange(1)
    gather(0)
    gather(1)
    low_copy.wait_send()
    for kind in range(2):
        for one in sum_copies(kind, 2):
            one.wait_recv()
        for step in range(3):
            for one in sum_copies(kind, step):
                one.wait_send()
        back_copy(kind).wait_send()

    def finish(h, carry):
        @pl.when(ctx + 2 < count)
        def _():
            far_copy(keys, 0, h).wait_send()
            far_copy(values, 1, h).wait_send()

        @pl.when((core == 0) | (ctx >= 2))
        def _():
            near_copy(keys, 0, h, 0, behind_1).wait_send()
            near_copy(values, 1, h, 0, behind_1).wait_send()

        @pl.when(ctx >= 1)
        def _():
            grad_copy(0, h).wait_send()

        @pl.when(ctx >= 2)
        def _():
            grad_copy(1, h).wait_send()

        out_copy(h).wait()
        return carry

    lax.fori_loop(0, KV, finish, 0)


def output_kernel(
    passed,
    final_query,
    final_value,
    attention_out,
    down_query,
    up_query,
    down_value,
    up_value,
    held,
    sums_query,
    sums_value,
    wide_0,
    wide_1,
    wide_2,
    wide_3,
    sem,
    sums_sem,
    wide_sem,
):
    size = TOKENS // PIECES

    def copy(k, step):
        piece = pl.ds(k * size, size)
        source, target = ((passed, held), (held, attention_out))[step]
        return pltpu.make_async_copy(source.at[piece], target.at[piece], sem.at[step, k])

    sums = [
        pltpu.make_async_copy(final_query, sums_query, sums_sem.at[0]),
        pltpu.make_async_copy(final_value, sums_value, sums_sem.at[1]),
    ]
    for one in sums:
        one.start()
    for k in range(PIECES):
        copy(k, 0).start()
    written = []
    for kind, (final, wides, outs) in enumerate(
        (
            (sums_query, (wide_0, wide_1), (down_query, up_query)),
            (sums_value, (wide_2, wide_3), (down_value, up_value)),
        )
    ):
        sums[kind].wait()
        width = final.shape[2]
        for which, at, chunk, inside, part in pieces_of([o.shape[1] for o in outs], width):
            wides[which][:, at : at + part] = final[chunk, :, inside : inside + part].astype(F32)
        for which in range(2):
            one = pltpu.make_async_copy(
                wides[which], outs[which], wide_sem.at[2 * kind + which]
            )
            one.start()
            written.append(one)
    for k in range(PIECES):
        copy(k, 0).wait()
        copy(k, 1).start()
    for k in range(PIECES):
        copy(k, 1).wait()
    for one in written:
        one.wait()


def per_device(
    hidden_states,
    query_base,
    key_base,
    frozen_value_rows,
    query_down,
    query_up,
    value_down,
    value_up_weight,
    positions,
    block_mask,
    output_gradient,
):
    anywhere = pl.BlockSpec(memory_space=pl.ANY)
    in_vmem = pl.BlockSpec(memory_space=pltpu.VMEM)
    columns = KV * HEAD_SIZE
    head_store = pltpu.VMEM((KV, REACH, HEAD_SIZE), BF16)
    value_terms = pltpu.VMEM((KV, 2, HEAD_SIZE, TOKENS), BF16)
    low_shape = pltpu.VMEM((2 * RANK, TOKENS), F32)
    query_sum = (GROUP, RANK, 5 * HEAD_SIZE)
    value_sum = (GROUP, RANK, 4 * HEAD_SIZE)
    dma = pltpu.SemaphoreType.DMA
    passed, final_query, final_value = pl.pallas_call(
        layer_kernel,
        out_shape=[
            jax.ShapeDtypeStruct((TOKENS, 2 * columns), BF16),
            jax.ShapeDtypeStruct(query_sum, BF16),
            jax.ShapeDtypeStruct(value_sum, BF16),
        ],
        in_specs=[anywhere] * 8
        + [in_vmem, in_vmem, pl.BlockSpec(memory_space=pltpu.SMEM), anywhere],
        out_specs=[anywhere, in_vmem, in_vmem],
        scratch_shapes=[
            pltpu.VMEM((TOKENS, FEATURES), BF16),
            pltpu.VMEM((TOKENS, 2 * columns), BF16),
            pltpu.VMEM((TOKENS, columns), BF16),
            pltpu.VMEM((TOKENS, columns), BF16),
            pltpu.VMEM((2 * RANK, FEATURES), BF16),
            pltpu.VMEM((2 * RANK, 2 * columns), BF16),
            pltpu.VMEM((2 * RANK, columns), BF16),
            pltpu.VMEM((TOKENS, 2 * columns), BF16),
            head_store,
            head_store,
            pltpu.VMEM((TOKENS, 2 * columns), BF16),
            pltpu.VMEM((TOKENS // ROWS, ROWS, SPAN), F32),
            pltpu.VMEM((TOKENS, HEAD_SIZE), F32),
            pltpu.VMEM((TOKENS, HEAD_SIZE), F32),
            low_shape,
            low_shape,
            pltpu.VMEM((2 * RANK, TOKENS), BF16),
            pltpu.VMEM((TOKENS, 2 * RANK), BF16),
            low_shape,
            low_shape,
            pltpu.VMEM((TOKENS, PAIR), BF16),
            pltpu.VMEM((2, TOKENS // ROWS, 2 * ROWS, SPAN), BF16),
            pltpu.VMEM((2, TOKENS // ROWS, 2 * ROWS, HEAD_SIZE), F32),
            pltpu.VMEM((HEAD_SIZE, REACH), F32),
            pltpu.VMEM((KV, HEAD_SIZE, TOKENS), F32),
            value_terms,
            value_terms,
            pltpu.VMEM((RANK, GROUP * query_sum[2]), F32),
            pltpu.VMEM((RANK, GROUP * value_sum[2]), F32),
        ]
        + [pltpu.VMEM(shape, BF16) for _ in range(3) for shape in (query_sum, value_sum)]
        + [
            dma((9,)),
            dma((KV,)),
            dma((2,)),
            dma((2, 2)),
        ]
        + [dma((2, KV))] * 6
        + [dma((2, 3, GROUP - 1))] * 2,
        compiler_params=pltpu.CompilerParams(
            collective_id=1, has_side_effects=True, vmem_limit_bytes=56 * 2**20
        ),
    )(
        hidden_states,
        query_base,
        key_base,
        frozen_value_rows,
        query_down.T,
        query_up,
        value_down.T,
        value_up_weight,
        positions.reshape(1, TOKENS),
        turns_of_angles(),
        block_mask.T,
        output_gradient,
    )
    outs = pl.pallas_call(
        output_kernel,
        out_shape=[
            jax.ShapeDtypeStruct((TOKENS, 2 * columns), BF16),
            jax.ShapeDtypeStruct((RANK, FEATURES), F32),
            jax.ShapeDtypeStruct((RANK, 2 * columns), F32),
            jax.ShapeDtypeStruct((RANK, FEATURES), F32),
            jax.ShapeDtypeStruct((RANK, columns), F32),
        ],
        in_specs=[anywhere] * 3,
        out_specs=[anywhere] * 5,
        scratch_shapes=[
            pltpu.VMEM((TOKENS, 2 * columns), BF16),
            pltpu.VMEM(query_sum, BF16),
            pltpu.VMEM(value_sum, BF16),
        ]
        + [pltpu.VMEM((RANK, width), F32) for width in (FEATURES, 2 * columns, FEATURES, columns)]
        + [dma((2, PIECES)), dma((2,)), dma((4,))],
        compiler_params=pltpu.CompilerParams(vmem_limit_bytes=56 * 2**20),
    )(passed, final_query, final_value)
    attention_out, down_query, up_query, down_value, up_value = outs
    return attention_out, down_query.T, up_query, down_value.T, up_value


def solution(mesh):
    placed = (
        P("ctx", "head"),
        P("ctx", "head"),
        P("ctx", "head"),
        P("ctx", "head"),
        P("head", None),
        P(None, "head"),
        P("head", None),
        P(None, "head"),
        P("ctx"),
        P(),
        P("ctx", "head"),
    )
    return jax.shard_map(
        per_device,
        mesh=mesh,
        in_specs=placed,
        out_specs=(
            P("ctx", "head"),
            P("head", None),
            P(None, "head"),
            P("head", None),
            P(None, "head"),
        ),
        check_vma=False,
    )
```

```python
import functools
import math

import jax
import jax.numpy as jnp
import numpy as np
from jax import lax
from jax.experimental import pallas as pl
from jax.experimental.pallas import tpu as pltpu
from jax.sharding import PartitionSpec as P

D = 5376
QUERY_HEADS = 32
KEY_VALUE_HEADS = 16
HEAD_SIZE = 128
WINDOW = 1024
BLOCK = 128
ROPE_BASE = 10000.0

TOKENS = 512
FEATURES = 2688
KV = 8
PAIR = 2 * HEAD_SIZE
ROWS = 256
SPAN = WINDOW + ROWS
REACH = WINDOW + TOKENS
AHEAD = 2
LAG = 3
HIDDEN = -1e30
SCALE = (D // QUERY_HEADS) ** -0.5
BF16 = jnp.bfloat16
F32 = jnp.float32

RANK = 16
GROUP = 8
PIECES = 4
MESH = pl.DeviceIdType.MESH


def pieces_of(widths, chunk_width):
    pieces, start = [], 0
    for which, width in enumerate(widths):
        done = 0
        while done < width:
            chunk, inside = divmod(start + done, chunk_width)
            size = min(width - done, chunk_width - inside)
            pieces.append((which, done, chunk, inside, size))
            done += size
        start += width
    return pieces


def turns_of_angles():
    half = HEAD_SIZE // 2
    turns = ROPE_BASE ** (-2.0 * np.arange(half) / HEAD_SIZE) / (2.0 * math.pi)
    mantissa, exponent = np.frexp(turns)
    coarse = np.ldexp(np.floor(mantissa * 256.0), exponent - 8)
    rows = np.stack([np.tile(coarse, 2), np.tile(turns - coarse, 2)])
    return np.concatenate([rows, np.zeros((6, HEAD_SIZE))]).astype(np.float32)


def nearest(x):
    return jnp.floor(x + 0.5)


def sine_of_turns(r):
    r = r - nearest(r)
    r = jnp.where(r > 0.25, 0.5 - r, jnp.where(r < -0.25, -0.5 - r, r))
    x = r * (2.0 * math.pi)
    y = x * x
    out = jnp.full_like(y, -1.0 / math.factorial(11))
    for power in (9, 7, 5, 3, 1):
        sign = 1.0 if power % 4 == 1 else -1.0
        out = out * y + sign / math.factorial(power)
    return out * x


def dot(a, b, contract):
    return lax.dot_general(a, b, ((contract[:1], contract[1:]), ((), ())), preferred_element_type=F32)


def layer_kernel(
    hidden_hbm,
    query_hbm,
    key_hbm,
    value_hbm,
    query_down_hbm,
    query_up_hbm,
    value_down_hbm,
    value_up_hbm,
    positions_ref,
    turns_ref,
    mask_ref,
    gradient_hbm,
    out_hbm,
    final_query,
    final_value,
    hidden,
    query_base,
    key_base,
    value_base,
    downs,
    query_up,
    value_up,
    gradient,
    keys,
    values,
    out,
    bias,
    cosines,
    sines,
    low_mine,
    low_theirs,
    low_rows,
    low_cols,
    back_mine,
    back_theirs,
    query_grad,
    held_weights,
    held_inverse,
    value_sum,
    value_own,
    value_sent,
    value_got,
    row_query,
    row_value,
    parts_query,
    parts_value,
    near_query,
    near_value,
    away_query,
    away_value,
    load_sem,
    out_sem,
    low_sem,
    back_sem,
    far_send,
    far_recv,
    near_send,
    near_recv,
    grad_send,
    grad_recv,
    sum_send,
    sum_recv,
):
    ctx, head = lax.axis_index("ctx"), lax.axis_index("head")
    count = lax.axis_size("ctx")
    core = ctx % 2
    ahead_1, ahead_2 = (ctx + 1) % count, (ctx + 2) % count
    behind_1, behind_2 = (ctx + count - 1) % count, (ctx + count - 2) % count

    def remote(source, target, send, recv, at_ctx, at_head=head):
        return pltpu.make_async_remote_copy(
            src_ref=source,
            dst_ref=target,
            send_sem=send,
            recv_sem=recv,
            device_id=(at_ctx, at_head),
            device_id_type=MESH,
        )

    loads = [
        pltpu.make_async_copy(source, target, load_sem.at[k])
        for k, (source, target) in enumerate(
            (
                (key_hbm, key_base),
                (query_down_hbm, downs.at[0:RANK]),
                (value_down_hbm, downs.at[RANK : 2 * RANK]),
                (hidden_hbm, hidden),
                (value_up_hbm, value_up.at[RANK : 2 * RANK]),
                (value_hbm, value_base),
                (query_up_hbm, query_up.at[0:RANK]),
                (query_hbm, query_base),
                (gradient_hbm, gradient),
            )
        )
    ]
    for one in loads:
        one.start()

    barrier = pltpu.get_barrier_semaphore()
    member, group = ctx % GROUP, ctx // GROUP
    groups = count // GROUP
    near_peers = [group * GROUP + (member + by) % GROUP for by in range(1, GROUP)]
    far_peers = [((group + by) % groups) * GROUP + member for by in range(1, groups)]
    greeted = [(at, head) for at in (ahead_1, ahead_2, behind_1, behind_2)]
    greeted += [(ctx, 1 - head)] + [(at, head) for at in near_peers + far_peers]
    for at in greeted:
        pl.semaphore_signal(barrier, inc=1, device_id=at, device_id_type=MESH)

    lane = lax.broadcasted_iota(jnp.int32, (TOKENS, HEAD_SIZE), 1)
    first_half = lane < HEAD_SIZE // 2
    position = jnp.transpose(
        jnp.broadcast_to(positions_ref[...].astype(F32), (HEAD_SIZE, TOKENS))
    )
    coarse = position * turns_ref[0:1, :]
    fine = position * turns_ref[1:2, :]
    turns = (coarse - nearest(coarse)) + (fine - nearest(fine))
    table = sine_of_turns(turns + jnp.where(first_half, 0.25, 0.0))
    swapped = pltpu.roll(table, HEAD_SIZE // 2, 1)
    cosines[...] = jnp.where(first_half, table, swapped)
    sines[...] = jnp.where(first_half, -swapped, table)

    def rope(x, cos, sin):
        return x * cos + pltpu.roll(x, HEAD_SIZE // 2, 1) * sin

    def turn_keys(h):
        columns = slice(h * HEAD_SIZE, (h + 1) * HEAD_SIZE)
        keys[h, WINDOW:REACH] = rope(
            key_base[:, columns].astype(F32), cosines[...], sines[...]
        ).astype(BF16)

    loads[0].wait()
    for h in range(AHEAD):
        turn_keys(h)

    pl.semaphore_wait(barrier, len(greeted))

    def far_copy(store, kind, h):
        return remote(
            store.at[h, WINDOW:REACH],
            store.at[h, 0:TOKENS],
            far_send.at[kind, h],
            far_recv.at[kind, h],
            ahead_2,
        )

    def near_copy(store, kind, h, first, at_ctx):
        return remote(
            store.at[h, pl.ds(first, TOKENS)],
            store.at[h, TOKENS:WINDOW],
            near_send.at[kind, h],
            near_recv.at[kind, h],
            at_ctx,
        )

    def send_own(store, kind, h):
        @pl.when(ctx + 2 < count)
        def _():
            far_copy(store, kind, h).start()

        @pl.when(core == 0)
        def _():
            near_copy(store, kind, h, WINDOW, ahead_1).start()

    for h in range(AHEAD):
        send_own(keys, 0, h)

    for one in loads[1:4]:
        one.wait()
    low_mine[...] = dot(downs[...], hidden[...], (1, 1))
    low_copy = remote(low_mine, low_theirs, low_sem.at[0], low_sem.at[1], ctx, 1 - head)
    low_copy.start()

    for h in range(AHEAD, KV):
        turn_keys(h)

    key_at = lax.broadcasted_iota(jnp.int32, (BLOCK, BLOCK), 1)
    query_at = lax.broadcasted_iota(jnp.int32, (BLOCK, BLOCK), 0)
    for half in range(TOKENS // ROWS):
        for r in range(ROWS // BLOCK):
            block = ctx * (TOKENS // BLOCK) + half * (ROWS // BLOCK) + r
            for j in range(SPAN // BLOCK):
                offset = WINDOW // BLOCK + r - j
                if 0 <= offset <= WINDOW // BLOCK:
                    seen = (mask_ref[offset, block] == 1) & (block >= offset)
                    tile = jnp.full((BLOCK, BLOCK), jnp.where(seen, 0.0, HIDDEN))
                    if offset == 0:
                        tile = jnp.where(key_at <= query_at, tile, HIDDEN)
                    if offset == WINDOW // BLOCK:
                        tile = jnp.where(key_at > query_at, tile, HIDDEN)
                else:
                    tile = jnp.full((BLOCK, BLOCK), HIDDEN, F32)
                bias[
                    half, r * BLOCK : (r + 1) * BLOCK, j * BLOCK : (j + 1) * BLOCK
                ] = tile

    query_up[RANK : 2 * RANK] = jnp.zeros((RANK, KV * PAIR), BF16)
    value_up[0:RANK] = jnp.zeros((RANK, KV * HEAD_SIZE), BF16)
    back_mine[...] = jnp.zeros_like(back_mine)
    for padded, used in ((row_query, FEATURES + KV * PAIR), (row_value, FEATURES + KV * HEAD_SIZE)):
        padded[:, used:] = jnp.zeros((RANK, padded.shape[1] - used), F32)

    @pl.when(ctx < 2)
    def _():
        for store in (keys, values):
            store[:, 0:TOKENS] = jnp.zeros((KV, TOKENS, HEAD_SIZE), BF16)

    @pl.when(ctx < 1)
    def _():
        for store in (keys, values):
            store[:, TOKENS:WINDOW] = jnp.zeros((KV, TOKENS, HEAD_SIZE), BF16)

    @pl.when(ctx + 2 >= count)
    def _():
        value_got[:, 1] = jnp.zeros((KV, HEAD_SIZE, TOKENS), BF16)

    @pl.when(ctx + 1 >= count)
    def _():
        value_got[:, 0] = jnp.zeros((KV, HEAD_SIZE, TOKENS), BF16)

    low_copy.wait_recv()
    low = low_mine[...] + low_theirs[...]
    low_rows[...] = low.astype(BF16)
    low_cols[...] = jnp.transpose(low).astype(BF16)
    loads[4].wait()
    loads[5].wait()
    for h in range(KV):
        columns = slice(h * HEAD_SIZE, (h + 1) * HEAD_SIZE)
        values[h, WINDOW:REACH] = (
            value_base[:, columns].astype(F32) + dot(low_cols[...], value_up[:, columns], (1, 0))
        ).astype(BF16)
        if h < AHEAD - 1:
            send_own(values, 1, h)
    for one in loads[6:]:
        one.wait()

    def out_copy(h):
        columns = pl.ds(pl.multiple_of(h * PAIR, PAIR), PAIR)
        return pltpu.make_async_copy(out.at[:, columns], out_hbm.at[:, columns], out_sem.at[h])

    def grad_copy(kind, h):
        return remote(
            value_sent.at[h, kind],
            value_got.at[h, kind],
            grad_send.at[kind, h],
            grad_recv.at[kind, h],
            behind_1 if kind == 0 else behind_2,
        )

    def stack(x):
        return jnp.concatenate([x[:, :HEAD_SIZE], x[:, HEAD_SIZE:]], axis=0)

    def beside(x):
        return jnp.concatenate([x[:ROWS], x[ROWS:]], axis=1)

    def send_terms(h):
        value_sent[h, 1] = value_sum[:, 0:TOKENS].astype(BF16)
        value_sent[h, 0] = value_sum[:, TOKENS:WINDOW].astype(BF16)

        @pl.when(ctx >= 2)
        def _():
            grad_copy(1, h).start()

        @pl.when(ctx >= 1)
        def _():
            grad_copy(0, h).start()

        value_own[h] = value_sum[:, WINDOW:REACH]

    halves = range(TOKENS // ROWS)
    rows = [slice(half * ROWS, (half + 1) * ROWS) for half in halves]
    span = [slice(half * ROWS, half * ROWS + SPAN) for half in halves]

    def twice(x):
        return jnp.concatenate([x, x], axis=0)

    def pair_of(h):
        return pl.ds(pl.multiple_of(h * PAIR, PAIR), PAIR)

    def key_part(h):
        pair = pair_of(h)

        def score(half):
            raw = query_base[rows[half], pair].astype(F32) + dot(
                low_cols[rows[half]], query_up[:, pair], (1, 0)
            )
            queries = rope(stack(raw), twice(cosines[rows[half]]), twice(sines[rows[half]]))
            queries = queries * (SCALE * math.log2(math.e))
            return dot(queries.astype(BF16), keys[h, span[half]], (1, 1))

        def weigh(half, scores):
            scores = (
                scores.reshape(2, ROWS, SPAN) + bias[half][None]
            ).reshape(2 * ROWS, SPAN)
            weights = jnp.exp2(scores - jnp.max(scores, axis=1, keepdims=True))
            inverse = 1.0 / jnp.sum(weights, axis=1, keepdims=True)
            weights = weights.astype(BF16)
            held_weights[h % 2, half] = weights
            held_inverse[h % 2, half] = jnp.broadcast_to(inverse, (2 * ROWS, HEAD_SIZE))
            out_grad = stack(gradient[rows[half], pair]).astype(F32)
            terms = dot((out_grad * inverse).astype(BF16), weights, (0, 0))
            if half == 0:
                value_sum[:, 0:SPAN] = terms
            else:
                value_sum[:, ROWS:SPAN] += terms[:, : SPAN - ROWS]
                value_sum[:, SPAN:REACH] = terms[:, SPAN - ROWS :]

        scores = [score(half) for half in halves]
        for half in halves:
            weigh(half, scores[half])
        send_terms(h)

    def value_part(h):
        pair = pair_of(h)

        def attend(half):
            result = dot(held_weights[h % 2, half], values[h, span[half]], (1, 0))
            result = (result * held_inverse[h % 2, half]).astype(BF16)
            out[rows[half], pair] = beside(result)
            return result

        def grad(half):
            return dot(stack(gradient[rows[half], pair]), values[h, span[half]], (1, 1))

        def back(half, grad_weights, result):
            out_grad = stack(gradient[rows[half], pair]).astype(F32)
            delta = jnp.sum(out_grad * result.astype(F32), axis=1, keepdims=True)
            grad_scores = held_weights[h % 2, half] * (grad_weights - delta).astype(BF16)
            turned = rope(
                dot(grad_scores, keys[h, span[half]], (1, 0))
                * (held_inverse[h % 2, half] * SCALE),
                twice(cosines[rows[half]]),
                -twice(sines[rows[half]]),
            )
            query_grad[rows[half]] = beside(turned.astype(BF16))

        results = [attend(half) for half in halves]
        grads = [grad(half) for half in halves]
        for half in halves:
            back(half, grads[half], results[half])
        out_copy(h).start()
        back_mine[0:RANK] += dot(query_up[0:RANK, pair], query_grad[...], (1, 1))
        row_query[:, pl.ds(pl.multiple_of(h * PAIR, HEAD_SIZE) + FEATURES, PAIR)] = dot(
            low_rows[0:RANK], query_grad[...], (1, 0)
        )

    def pass_on(store, kind, h):
        @pl.when(ctx >= 2)
        def _():
            far_copy(store, kind, h).wait_recv()

        @pl.when((core == 1) & (ctx >= 2))
        def _():
            near_copy(store, kind, h, 0, behind_1).start()

    def arrived(store, kind, h):
        @pl.when(ctx >= 1)
        def _():
            near_copy(store, kind, h, 0, behind_1).wait_recv()

    def absorb(h):
        @pl.when(ctx + 1 < count)
        def _():
            grad_copy(0, h).wait_recv()

        @pl.when(ctx + 2 < count)
        def _():
            grad_copy(1, h).wait_recv()

        total = (
            value_own[h] + value_got[h, 0].astype(F32) + value_got[h, 1].astype(F32)
        ).astype(BF16)
        columns = pl.ds(pl.multiple_of(h * HEAD_SIZE, HEAD_SIZE), HEAD_SIZE)
        back_mine[RANK : 2 * RANK] += dot(value_up[RANK : 2 * RANK, columns], total, (1, 0))
        row_value[:, pl.ds(pl.multiple_of(h * HEAD_SIZE, HEAD_SIZE) + FEATURES, HEAD_SIZE)] = dot(
            low_rows[RANK : 2 * RANK], total, (1, 1)
        )

    def one_head(h, carry):
        @pl.when(h + AHEAD < KV)
        def _():
            send_own(keys, 0, h + AHEAD)

        @pl.when(h + AHEAD - 1 < KV)
        def _():
            send_own(values, 1, h + AHEAD - 1)

        pass_on(keys, 0, h)
        arrived(keys, 0, h)
        key_part(h)

        @pl.when(h >= 1)
        def _():
            pass_on(values, 1, h - 1)
            arrived(values, 1, h - 1)
            value_part(h - 1)

        @pl.when(h >= LAG)
        def _():
            absorb(h - LAG)

        return carry

    lax.fori_loop(0, KV, one_head, 0)
    pass_on(values, 1, KV - 1)

    def back_copy(kind):
        rows = pl.ds(kind * RANK, RANK)
        return remote(
            back_mine.at[rows],
            back_theirs.at[rows],
            back_sem.at[0, kind],
            back_sem.at[1, kind],
            ctx,
            1 - head,
        )

    stores = (
        (row_query, parts_query, near_query, away_query, final_query),
        (row_value, parts_value, near_value, away_value, final_value),
    )

    def sum_copy(kind, step, k, peer):
        _, parts, near, away, final = stores[kind]
        source, target = (
            (parts.at[peer % GROUP], near.at[k]),
            (away.at[group], away.at[group]),
            (final.at[member], final.at[member]),
        )[step]
        return remote(
            source, target, sum_send.at[kind, step, k], sum_recv.at[kind, step, k], peer
        )

    def sum_copies(kind, step):
        peers = far_peers if step == 1 else near_peers
        return [sum_copy(kind, step, k, peer) for k, peer in enumerate(peers)]

    def scatter(kind):
        row, parts = stores[kind][:2]
        rows = slice(kind * RANK, (kind + 1) * RANK)
        back_copy(kind).wait_recv()
        total = (back_mine[rows] + back_theirs[rows]).astype(BF16)
        row[:, 0:FEATURES] = dot(total, hidden[...], (1, 0))
        width = parts.shape[2]
        for k in range(GROUP):
            parts[k] = row[:, k * width : (k + 1) * width].astype(BF16)
        for one in sum_copies(kind, 0):
            one.start()

    def exchange(kind):
        _, parts, near, away, _ = stores[kind]
        total = parts[member].astype(F32)
        for k, one in enumerate(sum_copies(kind, 0)):
            one.wait_recv()
            total += near[k].astype(F32)
        away[group] = total.astype(BF16)
        for one in sum_copies(kind, 1):
            one.start()

    def gather(kind):
        away, final = stores[kind][3:]
        for one in sum_copies(kind, 1):
            one.wait_recv()
        total = away[0].astype(F32)
        for k in range(1, groups):
            total += away[k].astype(F32)
        final[member] = (total * (TOKENS * count) ** -0.5).astype(BF16)
        for one in sum_copies(kind, 2):
            one.start()

    for h in range(KV - LAG, KV - 1):
        absorb(h)
    absorb(KV - 1)
    back_copy(1).start()
    arrived(values, 1, KV - 1)
    value_part(KV - 1)
    back_copy(0).start()
    scatter(1)
    scatter(0)
    exchange(1)
    exchange(0)
    gather(1)
    gather(0)
    low_copy.wait_send()
    for kind in range(2):
        for one in sum_copies(kind, 2):
            one.wait_recv()
        for step in range(3):
            for one in sum_copies(kind, step):
                one.wait_send()
        back_copy(kind).wait_send()

    def finish(h, carry):
        @pl.when(ctx + 2 < count)
        def _():
            far_copy(keys, 0, h).wait_send()
            far_copy(values, 1, h).wait_send()

        @pl.when((core == 0) | (ctx >= 2))
        def _():
            near_copy(keys, 0, h, 0, behind_1).wait_send()
            near_copy(values, 1, h, 0, behind_1).wait_send()

        @pl.when(ctx >= 1)
        def _():
            grad_copy(0, h).wait_send()

        @pl.when(ctx >= 2)
        def _():
            grad_copy(1, h).wait_send()

        out_copy(h).wait()
        return carry

    lax.fori_loop(0, KV, finish, 0)


def output_kernel(
    passed,
    final_query,
    final_value,
    attention_out,
    down_query,
    up_query,
    down_value,
    up_value,
    held,
    sums_query,
    sums_value,
    wide_0,
    wide_1,
    wide_2,
    wide_3,
    sem,
    sums_sem,
    wide_sem,
):
    size = TOKENS // PIECES

    def copy(k, step):
        piece = pl.ds(k * size, size)
        source, target = ((passed, held), (held, attention_out))[step]
        return pltpu.make_async_copy(source.at[piece], target.at[piece], sem.at[step, k])

    sums = [
        pltpu.make_async_copy(final_query, sums_query, sums_sem.at[0]),
        pltpu.make_async_copy(final_value, sums_value, sums_sem.at[1]),
    ]
    for one in sums:
        one.start()
    for k in range(PIECES):
        copy(k, 0).start()
    written = []
    for kind, (final, wides, outs) in enumerate(
        (
            (sums_query, (wide_0, wide_1), (down_query, up_query)),
            (sums_value, (wide_2, wide_3), (down_value, up_value)),
        )
    ):
        sums[kind].wait()
        width = final.shape[2]
        for which, at, chunk, inside, part in pieces_of([o.shape[1] for o in outs], width):
            wides[which][:, at : at + part] = final[chunk, :, inside : inside + part].astype(F32)
        for which in range(2):
            one = pltpu.make_async_copy(
                wides[which], outs[which], wide_sem.at[2 * kind + which]
            )
            one.start()
            written.append(one)
    for k in range(PIECES):
        copy(k, 0).wait()
        copy(k, 1).start()
    for k in range(PIECES):
        copy(k, 1).wait()
    for one in written:
        one.wait()


def per_device(
    hidden_states,
    query_base,
    key_base,
    frozen_value_rows,
    query_down,
    query_up,
    value_down,
    value_up_weight,
    positions,
    block_mask,
    output_gradient,
):
    anywhere = pl.BlockSpec(memory_space=pl.ANY)
    in_vmem = pl.BlockSpec(memory_space=pltpu.VMEM)
    columns = KV * HEAD_SIZE
    head_store = pltpu.VMEM((KV, REACH, HEAD_SIZE), BF16)
    value_terms = pltpu.VMEM((KV, 2, HEAD_SIZE, TOKENS), BF16)
    low_shape = pltpu.VMEM((2 * RANK, TOKENS), F32)
    query_sum = (GROUP, RANK, 5 * HEAD_SIZE)
    value_sum = (GROUP, RANK, 4 * HEAD_SIZE)
    dma = pltpu.SemaphoreType.DMA
    passed, final_query, final_value = pl.pallas_call(
        layer_kernel,
        out_shape=[
            jax.ShapeDtypeStruct((TOKENS, 2 * columns), BF16),
            jax.ShapeDtypeStruct(query_sum, BF16),
            jax.ShapeDtypeStruct(value_sum, BF16),
        ],
        in_specs=[anywhere] * 8
        + [in_vmem, in_vmem, pl.BlockSpec(memory_space=pltpu.SMEM), anywhere],
        out_specs=[anywhere, in_vmem, in_vmem],
        scratch_shapes=[
            pltpu.VMEM((TOKENS, FEATURES), BF16),
            pltpu.VMEM((TOKENS, 2 * columns), BF16),
            pltpu.VMEM((TOKENS, columns), BF16),
            pltpu.VMEM((TOKENS, columns), BF16),
            pltpu.VMEM((2 * RANK, FEATURES), BF16),
            pltpu.VMEM((2 * RANK, 2 * columns), BF16),
            pltpu.VMEM((2 * RANK, columns), BF16),
            pltpu.VMEM((TOKENS, 2 * columns), BF16),
            head_store,
            head_store,
            pltpu.VMEM((TOKENS, 2 * columns), BF16),
            pltpu.VMEM((TOKENS // ROWS, ROWS, SPAN), F32),
            pltpu.VMEM((TOKENS, HEAD_SIZE), F32),
            pltpu.VMEM((TOKENS, HEAD_SIZE), F32),
            low_shape,
            low_shape,
            pltpu.VMEM((2 * RANK, TOKENS), BF16),
            pltpu.VMEM((TOKENS, 2 * RANK), BF16),
            low_shape,
            low_shape,
            pltpu.VMEM((TOKENS, PAIR), BF16),
            pltpu.VMEM((2, TOKENS // ROWS, 2 * ROWS, SPAN), BF16),
            pltpu.VMEM((2, TOKENS // ROWS, 2 * ROWS, HEAD_SIZE), F32),
            pltpu.VMEM((HEAD_SIZE, REACH), F32),
            pltpu.VMEM((KV, HEAD_SIZE, TOKENS), F32),
            value_terms,
            value_terms,
            pltpu.VMEM((RANK, GROUP * query_sum[2]), F32),
            pltpu.VMEM((RANK, GROUP * value_sum[2]), F32),
        ]
        + [pltpu.VMEM(shape, BF16) for _ in range(3) for shape in (query_sum, value_sum)]
        + [
            dma((9,)),
            dma((KV,)),
            dma((2,)),
            dma((2, 2)),
        ]
        + [dma((2, KV))] * 6
        + [dma((2, 3, GROUP - 1))] * 2,
        compiler_params=pltpu.CompilerParams(
            collective_id=1, has_side_effects=True, vmem_limit_bytes=56 * 2**20
        ),
    )(
        hidden_states,
        query_base,
        key_base,
        frozen_value_rows,
        query_down.T,
        query_up,
        value_down.T,
        value_up_weight,
        positions.reshape(1, TOKENS),
        turns_of_angles(),
        block_mask.T,
        output_gradient,
    )
    outs = pl.pallas_call(
        output_kernel,
        out_shape=[
            jax.ShapeDtypeStruct((TOKENS, 2 * columns), BF16),
            jax.ShapeDtypeStruct((RANK, FEATURES), F32),
            jax.ShapeDtypeStruct((RANK, 2 * columns), F32),
            jax.ShapeDtypeStruct((RANK, FEATURES), F32),
            jax.ShapeDtypeStruct((RANK, columns), F32),
        ],
        in_specs=[anywhere] * 3,
        out_specs=[anywhere] * 5,
        scratch_shapes=[
            pltpu.VMEM((TOKENS, 2 * columns), BF16),
            pltpu.VMEM(query_sum, BF16),
            pltpu.VMEM(value_sum, BF16),
        ]
        + [pltpu.VMEM((RANK, width), F32) for width in (FEATURES, 2 * columns, FEATURES, columns)]
        + [dma((2, PIECES)), dma((2,)), dma((4,))],
        compiler_params=pltpu.CompilerParams(vmem_limit_bytes=56 * 2**20),
    )(passed, final_query, final_value)
    attention_out, down_query, up_query, down_value, up_value = outs
    return attention_out, down_query.T, up_query, down_value.T, up_value


def solution(mesh):
    placed = (
        P("ctx", "head"),
        P("ctx", "head"),
        P("ctx", "head"),
        P("ctx", "head"),
        P("head", None),
        P(None, "head"),
        P("head", None),
        P(None, "head"),
        P("ctx"),
        P(),
        P("ctx", "head"),
    )
    return jax.shard_map(
        per_device,
        mesh=mesh,
        in_specs=placed,
        out_specs=(
            P("ctx", "head"),
            P("head", None),
            P(None, "head"),
            P("head", None),
            P(None, "head"),
        ),
        check_vma=False,
    )
```
